256 devices in a mesh: flow: 16 (over x_lo, z), trans: 16 (over y, x_hi, core).
Axes of the slice: x: 4 (x_hi: 2, x_lo: 2; x = x_hi * 2 + x_lo), y: 4, z: 8, core: 2. Of those that a mesh axis runs over, the one named last changes fastest.
Arguments:
- populations: float32 [19, 384, 256, 256], P(None, 'flow', 'trans'), may hold values from 0.016666667 to 0.46666667, as said below
- magnetization: float32 [2, 2, 384, 256, 256], P(None, None, 'flow', 'trans'), may hold values from -6 to 6
- pore: int32 [384, 256, 256], P('flow', 'trans'), may hold values 0 or 1
- wall: int32 [384, 256, 256], P('flow', 'trans'), may hold values 0 or 1
Outputs:
- velocity: float32 [3, 384, 256, 256], P(None, 'flow', 'trans')
- new_magnetization: float32 [2, 2, 384, 256, 256], P(None, None, 'flow', 'trans')
- signal: float32 [2, 2], replicated
The draws below stay inside these ranges and needn't reach their ends.
Inputs may be any that keep to these rules, and one draw needn't show every extreme that they name: `populations`: population i is its lattice weight times a factor between 0.6 and 1.4.
All inputs are finite; a program needn't handle non-finite values. No bound on the sum of `pore` or of `wall` on one device may be relied on, other than what follows from the above.
Results may differ from the reference program's by a relative error of at most 0.000025.
Values sent between devices are 32-bit elements; how exact they have to be, the bound alone decides.
No kernel may reach another device: no remote copies, remote signals or barrier semaphores. Data moves between devices by JAX's collectives and lax.ppermute only.
A program may use at most 128 MiB of HBM per device.

```python
import math
import jax
import jax.numpy as jnp
from jax import lax

NX = 256
Q_LOW = 2
Q_HIGH = 5
NZ = 384
NY = 256


def draw_populations(key, part):
    key = jax.random.fold_in(key, 11)
    weights = jnp.array([1.0 / 3.0] + [1.0 / 18.0] * 6 + [1.0 / 36.0] * 12, jnp.float32)
    factor = 1.0 + 0.15 * jax.random.truncated_normal(key, -2.6, 2.6, (19, NZ, NY, NX), jnp.float32)
    return (weights[:, None, None, None] * factor).astype(jnp.float32)


def plant(result, key, least, high):
    shape = result.shape
    place = [jax.random.randint(jax.random.fold_in(key, axis), (), 0, shape[axis]) for axis in range(len(shape))]
    result = result.at[tuple(place)].set(least)
    longest = shape.index(max(shape))
    place[longest] = (place[longest] + 1) % shape[longest]
    return result.at[tuple(place)].set(high)


def block_levels(stream_key, shape, pieces, smallest, high):
    def one(position, shards_of):
        draws = jax.random.uniform(jax.random.fold_in(jax.random.fold_in(stream_key, 6), position), (shards_of,), jnp.float32, smallest / len(pieces), high / len(pieces))
        return jnp.repeat(jnp.exp(draws), shape[position] // shards_of).reshape((-1,) + (1,) * (len(shape) - position - 1))

    factor_of = one(*pieces[0])
    for cut in pieces[1:]:
        factor_of = factor_of * one(*cut)
    return factor_of


def normal_values(key, shape, deviation, most, pieces=(), kind=jnp.bfloat16):
    result = deviation * jax.random.normal(key, shape, jnp.float32)
    if pieces:
        result = result * block_levels(key, shape, pieces, -0.22, 0.18)
    return jnp.clip(result, -most, most).astype(kind)


def setup_inputs(seed: int = 0) -> dict:
    key_list = jax.random.split(jax.random.key(seed), 5)
    populations = draw_populations(jax.random.fold_in(key_list[4], 71), 0)
    magnetization = normal_values(key_list[1], (2, 2, NZ, NY, NX), 1.0, 6.0, ((2, 16), (3, 16)), jnp.float32)
    pore = plant((jax.random.randint(key_list[2], (NZ, NY, NX), 0, 4) < 3).astype(jnp.int32), jax.random.fold_in(key_list[2], 1), 0, 1)
    wall = plant((jax.random.randint(key_list[3], (NZ, NY, NX), 0, 4) < 1).astype(jnp.int32), jax.random.fold_in(key_list[3], 1), 0, 1)
    return {"populations": populations, "magnetization": magnetization, "pore": pore, "wall": wall}


VELOCITIES = ((0, 0, 0), (1, 0, 0), (-1, 0, 0), (0, 1, 0), (0, -1, 0), (0, 0, 1), (0, 0, -1), (1, 1, 0), (-1, -1, 0), (1, -1, 0), (-1, 1, 0), (1, 0, 1), (-1, 0, -1), (1, 0, -1), (-1, 0, 1), (0, 1, 1), (0, -1, -1), (0, 1, -1), (0, -1, 1))
WEIGHTS = (1.0 / 3.0,) + (1.0 / 18.0,) * 6 + (1.0 / 36.0,) * 12
OPPOSITE = (0, 2, 1, 4, 3, 6, 5, 8, 7, 10, 9, 12, 11, 14, 13, 16, 15, 18, 17)
relax_time = 1.25
body_force = 0.002
diffusion_step = 0.1
surface_relax = 0.4

def add_moments(totals, shifted, pop_index):
    step_z, step_y, step_x = VELOCITIES[pop_index]
    density, mom_z, mom_y, mom_x = totals
    return (density + shifted, mom_z + step_z * shifted, mom_y + step_y * shifted, mom_x + step_x * shifted)

def moments(pops_in):
    zeros_grid = jnp.zeros_like(pops_in[0])
    totals = (zeros_grid, zeros_grid, zeros_grid, zeros_grid)
    for pop_index in range(19):
        totals = add_moments(totals, pops_in[pop_index], pop_index)
    return totals

def collide_one(pops_in, pop_index, density, vel_z, vel_y, vel_x, speed_sq, pore_f):
    step_z, step_y, step_x = VELOCITIES[pop_index]
    dotted = step_z * vel_z + step_y * vel_y + step_x * vel_x
    equilibrium = WEIGHTS[pop_index] * density * (1.0 + 3.0 * dotted + 4.5 * dotted * dotted - 1.5 * speed_sq)
    relaxed = pops_in[pop_index] - (pops_in[pop_index] - equilibrium) / relax_time
    return jnp.where(pore_f > 0.5, relaxed, pops_in[OPPOSITE[pop_index]])

def flow_fields(pops_in):
    density, mom_z, mom_y, mom_x = moments(pops_in)
    vel_z = mom_z / density + relax_time * body_force
    vel_y = mom_y / density
    vel_x = mom_x / density
    speed_sq = vel_z * vel_z + vel_y * vel_y + vel_x * vel_x
    return (density, vel_z, vel_y, vel_x, speed_sq)

def phase_tables(coords_int, extent):
    coords = coords_int.astype(jnp.float32)
    wave_numbers = jnp.array([Q_LOW, Q_HIGH], jnp.float32)
    angles = 2.0 * math.pi * wave_numbers[:, None] * coords[None, :] / extent
    return (jnp.cos(angles)[:, :, None, None], jnp.sin(angles)[:, :, None, None])

def torrey_step(extended, vel, pore_f, wall_f, cos_z, sin_z):
    center = extended[:, :, 1:-1, 1:-1]
    plus_z = extended[:, :, 2:, 1:-1]
    minus_z = extended[:, :, :-2, 1:-1]
    plus_y = extended[:, :, 1:-1, 2:]
    minus_y = extended[:, :, 1:-1, :-2]
    plus_x = jnp.roll(center, -1, axis=4)
    minus_x = jnp.roll(center, 1, axis=4)
    laplace = plus_z + minus_z + plus_y + minus_y + plus_x + minus_x - 6.0 * center
    advect = 0.5 * (vel[0] * (plus_z - minus_z) + vel[1] * (plus_y - minus_y) + vel[2] * (plus_x - minus_x))
    updated = center + diffusion_step * laplace - advect - surface_relax * wall_f * center
    real_part = updated[:, 0]
    imag_part = updated[:, 1]
    rot_real = real_part * cos_z + imag_part * sin_z
    rot_imag = imag_part * cos_z - real_part * sin_z
    return jnp.stack([rot_real, rot_imag], axis=1) * pore_f

def reference(populations, magnetization, pore, wall):
    pore_f = pore.astype(jnp.float32)
    wall_f = wall.astype(jnp.float32)
    density, vel_z, vel_y, vel_x, speed_sq = flow_fields(populations)
    zeros_grid = jnp.zeros_like(density)
    totals = (zeros_grid, zeros_grid, zeros_grid, zeros_grid)
    for pop_index in range(19):
        relaxed = collide_one(populations, pop_index, density, vel_z, vel_y, vel_x, speed_sq, pore_f)
        step_z, step_y, step_x = VELOCITIES[pop_index]
        shifted = jnp.roll(relaxed, (step_z, step_y, step_x), axis=(0, 1, 2))
        totals = add_moments(totals, shifted, pop_index)
    new_density, mom_z, mom_y, mom_x = totals
    velocity = pore_f * jnp.stack([mom_z, mom_y, mom_x]) / new_density
    cos_z, sin_z = phase_tables(jnp.arange(NZ, dtype=jnp.int32), NZ)
    magnet = magnetization
    for sweep in range(2):
        extended = jnp.pad(magnet, ((0, 0), (0, 0), (1, 1), (1, 1), (0, 0)), mode='wrap')
        magnet = torrey_step(extended, velocity, pore_f, wall_f, cos_z, sin_z)
    signal = lax.optimization_barrier(jnp.sum(magnet, axis=(2, 3, 4))) / math.sqrt(NZ * NY * NX)
    return (velocity, magnet, signal)
```

```python
import functools
import math

import jax
import jax.numpy as jnp
from jax import lax
from jax.experimental import pallas as pl
from jax.experimental.pallas import tpu as pltpu
from jax.sharding import PartitionSpec as P

Q_LOW = 2
Q_HIGH = 5
RELAX_TIME = 1.25
BODY_FORCE = 0.002
DIFFUSION = 0.1
SURFACE = 0.4
BLOCK = 4
PLANES = 18


VMEM_LIMIT = 48 * 1024 * 1024


def row_mask(shape, row):
    return lax.broadcasted_iota(jnp.int32, shape, 0) == row


def collide_layer(pop, pore):
    p0 = pop(0)
    sums = []
    diffs = []
    for pair in range(9):
        fwd = pop(2 * pair + 1)
        bwd = pop(2 * pair + 2)
        sums.append(fwd + bwd)
        diffs.append(fwd - bwd)
    density = p0
    for s in sums:
        density = density + s
    mom_z = diffs[0] + diffs[3] + diffs[4] + diffs[5] + diffs[6]
    mom_y = diffs[1] + diffs[3] - diffs[4] + diffs[7] + diffs[8]
    mom_x = diffs[2] + diffs[5] - diffs[6] + diffs[7] - diffs[8]
    inv = 1.0 / density
    u_z = mom_z * inv + RELAX_TIME * BODY_FORCE
    u_y = mom_y * inv
    u_x = mom_x * inv
    is_pore = pore > 0
    rate = 1.0 / RELAX_TIME
    keep_s = jnp.where(is_pore, 0.5 * (1.0 - rate), 0.5)
    keep_d = jnp.where(is_pore, 0.5 * (1.0 - rate), -0.5)
    scaled = jnp.where(is_pore, density * (rate / 36.0), 0.0)
    h_z, h_y, h_x = scaled * u_z, scaled * u_y, scaled * u_x
    q_zz, q_yy, q_xx = 4.5 * h_z * u_z, 4.5 * h_y * u_y, 4.5 * h_x * u_x
    base = scaled - (q_zz + q_yy + q_xx) * (1.0 / 3.0)
    m_z, m_y, m_x = 3.0 * h_z, 3.0 * h_y, 3.0 * h_x
    q_zy, q_zx, q_yx = 3.0 * m_z * u_y, 3.0 * m_z * u_x, 3.0 * m_y * u_x
    out = [(keep_s + keep_s) * p0 + 12.0 * base]
    evens = [
        2.0 * (base + q_zz),
        2.0 * (base + q_yy),
        2.0 * (base + q_xx),
    ]
    zy = base + q_zz + q_yy
    zx = base + q_zz + q_xx
    yx = base + q_yy + q_xx
    evens += [zy + q_zy, zy - q_zy, zx + q_zx, zx - q_zx, yx + q_yx, yx - q_yx]
    odds = [2.0 * m_z, 2.0 * m_y, 2.0 * m_x, m_z + m_y, m_z - m_y, m_z + m_x, m_z - m_x, m_y + m_x, m_y - m_x]
    for pair in range(9):
        even = keep_s * sums[pair] + evens[pair]
        odd = keep_d * diffs[pair] + odds[pair]
        out.append(even + odd)
        out.append(even - odd)
    return out


def collide_kernel(pops, pore, m_low, m_high, pore_low, pore_high, wall_low, wall_high, acc, rows, up, down):
    step = pl.program_id(0)
    layers = pops.shape[1]
    width = pops.shape[2]
    total = acc.shape[1]
    shape = pops.shape[2:]

    @pl.when(step == 0)
    def _():
        acc[:, 0:2] = jnp.zeros((4, 2) + shape, jnp.float32)

    top = row_mask(shape, 0)
    bottom = row_mask(shape, width - 1)

    def layer(index, carry):
        z = step * layers + index
        r = collide_layer(lambda i: pops[i, index], pore[index])
        for i, sign in ((5, 1), (11, 1), (14, 1), (15, 1), (18, 1), (6, -1), (12, -1), (13, -1), (16, -1), (17, -1)):
            r[i] = pltpu.roll(r[i], sign % shape[1], 1)

        def shift_y(value, side):
            turned = pltpu.roll(value, 1 if side == 0 else width - 1, 0)
            return jnp.where(top if side == 0 else bottom, 0.0, turned)

        moved = []
        for side, (plain, x_up, x_down, z_up, z_down) in enumerate(((3, 15, 17, 7, 10), (4, 18, 16, 9, 8))):
            edge = width - 1 if side == 0 else 0
            both = r[plain] + r[x_up] + r[x_down]
            diff = r[x_up] - r[x_down]
            for slot, value in enumerate((both, diff, r[z_up], r[z_down])):
                rows[side, slot, pl.ds(z, 1), :] = value[edge : edge + 1]
            moved.append([shift_y(value, side) for value in (both, diff, r[z_up], r[z_down])])
        (up_d, up_x, up_zu, up_zd), (dn_d, dn_x, dn_zu, dn_zd) = moved
        acc[0, z + 2] = r[1] + r[11] + r[13] + up_zu + dn_zu
        acc[1, z + 2] = acc[0, z + 2]
        acc[2, z + 2] = up_zu - dn_zu
        acc[3, z + 2] = r[11] - r[13]
        acc[0, z + 1] = acc[0, z + 1] + (r[0] + r[5] + r[6] + up_d + dn_d)
        acc[2, z + 1] = acc[2, z + 1] + (up_d - dn_d)
        acc[3, z + 1] = acc[3, z + 1] + (r[5] - r[6] + up_x + dn_x)
        below = r[2] + r[12] + r[14] + up_zd + dn_zd
        acc[0, z] = acc[0, z] + below
        acc[1, z] = acc[1, z] - below
        acc[2, z] = acc[2, z] + (up_zd - dn_zd)
        acc[3, z] = acc[3, z] + (r[14] - r[12])
        return carry

    lax.fori_loop(0, layers, layer, 0)

    @pl.when(step == pl.num_programs(0) - 1)
    def _():
        last = total - 2
        for face, cross, own, near, far, pore_at, wall_at, z_row, diag in (
            (up, total - 1, last, m_high[:, 1], m_high[:, 0], pore_high, wall_high, last - 1, 2),
            (down, 0, 1, m_low[:, 0], m_low[:, 1], pore_low, wall_low, 0, 3),
        ):
            face[0] = acc[0, cross]
            face[1] = acc[2, cross]
            face[2] = acc[3, cross]
            face[3:7] = acc[:, own]
            face[7:11] = near
            face[11:15] = far
            face[15] = pore_at[0].astype(jnp.float32)
            face[16] = wall_at[0].astype(jnp.float32)
            inner = z_row - 1 if face is up else z_row + 1
            for side in range(2):
                at = 4 * side
                both = rows[side, 0, z_row : z_row + 1, :]
                diff = rows[side, 1, z_row : z_row + 1, :]
                along = rows[side, diag, inner : inner + 1, :]
                face[17, at : at + 1, :] = rows[side, diag, z_row : z_row + 1, :]
                face[17, at + 1 : at + 2, :] = both + along
                face[17, at + 2 : at + 3, :] = along if face is up else -along
                face[17, at + 3 : at + 4, :] = diff


def pack_kernel(acc, rows, magnet, pore, wall, up, down):
    depth = rows.shape[2]
    width = magnet.shape[2]
    first = row_mask((depth, rows.shape[3]), 0)
    final = row_mask((depth, rows.shape[3]), depth - 1)
    for side, face in ((0, up), (1, down)):
        from_below = jnp.where(first, 0.0, pltpu.roll(rows[side, 2], 1, 0))
        from_above = jnp.where(final, 0.0, pltpu.roll(rows[side, 3], depth - 1, 0))
        face[0] = rows[side, 0] + from_below + from_above
        face[1] = from_below - from_above
        face[2] = rows[side, 1]
        face[17] = jnp.zeros_like(face[17])

    def layer(z, carry):
        for face, near, far in ((up, width - 1, width - 2), (down, 0, 1)):
            at = pl.ds(z, 1)
            for k in range(4):
                face[3 + k, at, :] = acc[k, z + 1, near : near + 1, :]
                face[7 + k, at, :] = magnet[k, z, near : near + 1, :]
                face[11 + k, at, :] = magnet[k, z, far : far + 1, :]
            face[15, at, :] = pore[z, near : near + 1, :].astype(jnp.float32)
            face[16, at, :] = wall[z, near : near + 1, :].astype(jnp.float32)
        return carry

    lax.fori_loop(0, depth, layer, 0)


def merge_kernel(low, high, acc, rows, up_in, down_in, up, down):
    up[...] = up_in[...]
    down[...] = down_in[...]
    depth = rows.shape[2]
    width = low.shape[1]
    for side, face, edge in ((0, up, width - 1), (1, down, 0)):
        at = 4 * side
        for halo, z, sign in ((low, 0, 1.0), (high, depth - 1, -1.0)):
            here = pl.ds(z, 1)
            diag = halo[17, at : at + 1, :]
            face[0, here, :] = face[0, here, :] + diag
            face[1, here, :] = face[1, here, :] + sign * diag
            cross = halo[0, edge : edge + 1, :]
            face[3, here, :] = face[3, here, :] + cross
            face[4, here, :] = face[4, here, :] + sign * cross
            face[5, here, :] = face[5, here, :] + halo[1, edge : edge + 1, :]
            face[6, here, :] = face[6, here, :] + halo[2, edge : edge + 1, :]
            slot = 3 if sign > 0 else 2
            mine = rows[side, slot, here, :]
            base = 0 if sign > 0 else 3
            face[17, base : base + 1, :] = halo[17, at + 1 : at + 2, :] + mine
            face[17, base + 1 : base + 2, :] = halo[17, at + 2 : at + 3, :] - sign * mine
            face[17, base + 2 : base + 3, :] = halo[17, at + 3 : at + 4, :]
            base = 6 if sign > 0 else 10
            for k in range(4):
                face[17, base + k : base + k + 1, :] = halo[7 + k, edge : edge + 1, :]


def coefficients(vel, pore, wall):
    half = [0.5 * v for v in vel]
    plain = DIFFUSION * pore
    center = (1.0 - 6.0 * DIFFUSION) * pore - SURFACE * (pore * wall)
    return center, [(plain - h, plain + h) for h in half]


def stencil(coef, center, z_pair, y_pair, x_width):
    mid, ((z_p, z_m), (y_p, y_m), (x_p, x_m)) = coef
    plus_x = pltpu.roll(center, x_width - 1, 1)
    minus_x = pltpu.roll(center, 1, 1)
    return (
        mid * center
        + (z_p * z_pair[0] + z_m * z_pair[1])
        + (y_p * y_pair[0] + y_m * y_pair[1])
        + (x_p * plus_x + x_m * minus_x)
    )


def rotate(values, cos, sin):
    out = []
    for k in range(2):
        re, im = values[2 * k], values[2 * k + 1]
        out.append(re * cos[k] + im * sin[k])
        out.append(im * cos[k] - re * sin[k])
    return out


def final_kernel(
    table, wide, acc, magnet, pore, wall, low, high, left, right, up, down, vel_out, mag_out, sums, mid, thin
):
    depth, width, x_width = pore.shape
    shape = (width, x_width)
    top = row_mask(shape, 0)
    bottom = row_mask(shape, width - 1)
    first = row_mask((depth, x_width), 0)
    final = row_mask((depth, x_width), depth - 1)

    for side, face, own, sign in ((0, left, down, -1.0), (1, right, up, 1.0)):
        density = face[3] + own[0]
        inv = 1.0 / density
        pore_f = face[15]
        scale = pore_f * inv
        vel = [
            (face[4] + own[1]) * scale,
            (face[5] + sign * own[0]) * scale,
            (face[6] + own[2]) * scale,
        ]
        coef = coefficients(vel, pore_f, face[16])
        cos = [jnp.concatenate([wide[k], wide[k]], axis=1) for k in range(2)]
        sin = [jnp.concatenate([wide[2 + k], wide[2 + k]], axis=1) for k in range(2)]
        values = []
        for k in range(4):
            center = face[7 + k]
            plus = jnp.where(final, face[17, 10 + k : 11 + k, :], pltpu.roll(center, depth - 1, 0))
            minus = jnp.where(first, face[17, 6 + k : 7 + k, :], pltpu.roll(center, 1, 0))
            far, near = face[11 + k], own[7 + k]
            y_pair = (near, far) if side == 0 else (far, near)
            values.append(stencil(coef, center, (plus, minus), y_pair, x_width))
        for k, value in enumerate(rotate(values, cos, sin)):
            thin[side, k] = value

    def phases(z):
        return [table[0, z + 1], table[1, z + 1]], [table[2, z + 1], table[3, z + 1]]

    def velocity(moments, cross_left, cross_right, pore_f):
        density, m_z, m_y, m_x = moments
        d_l, z_l, x_l = cross_left
        d_r, z_r, x_r = cross_right
        density = density + jnp.where(top, d_l, jnp.where(bottom, d_r, 0.0))
        m_z = m_z + jnp.where(top, z_l, jnp.where(bottom, z_r, 0.0))
        m_y = m_y + jnp.where(top, d_l, jnp.where(bottom, -d_r, 0.0))
        m_x = m_x + jnp.where(top, x_l, jnp.where(bottom, x_r, 0.0))
        scale = pore_f / density
        return [m_z * scale, m_y * scale, m_x * scale]

    def beside(center, row_low, row_high):
        plus = jnp.where(bottom, row_high, pltpu.roll(center, width - 1, 0))
        minus = jnp.where(top, row_low, pltpu.roll(center, 1, 0))
        return plus, minus

    def first_step(z, vel, pore_f, wall_f, center, plus, minus, row_low, row_high):
        coef = coefficients(vel, pore_f, wall_f)
        cos, sin = phases(z)
        values = [
            stencil(coef, center(k), (plus(k), minus(k)), beside(center(k), row_low(k), row_high(k)), x_width)
            for k in range(4)
        ]
        for k, value in enumerate(rotate(values, cos, sin)):
            mid[k, z + 1] = value

    def halo_layer(halo, z, sign):
        cross = 0 if z < 0 else depth + 1
        moments = [
            halo[3] + acc[0, cross],
            halo[4] + acc[1, cross],
            halo[5] + acc[2, cross],
            halo[6] + acc[3, cross],
        ]
        base = 0 if z < 0 else 3
        vel = velocity(
            moments,
            [left[17, base + j : base + j + 1, :] for j in range(3)],
            [right[17, base + j : base + j + 1, :] for j in range(3)],
            halo[15],
        )
        corner = 6 if z < 0 else 10
        inside = 0 if z < 0 else depth - 1
        near, far = (lambda k: magnet[k, inside]), (lambda k: halo[11 + k])
        first_step(
            z,
            vel,
            halo[15],
            halo[16],
            lambda k: halo[7 + k],
            near if z < 0 else far,
            far if z < 0 else near,
            lambda k: left[17, corner + k : corner + k + 1, :],
            lambda k: right[17, corner + k : corner + k + 1, :],
        )

    def own_layer(z, extra, plus, minus):
        at = pl.ds(z, 1)
        moments = [acc[k, z + 1] for k in range(4)]
        if extra is not None:
            halo, sign = extra
            moments = [
                moments[0] + halo[0],
                moments[1] + sign * halo[0],
                moments[2] + halo[1],
                moments[3] + halo[2],
            ]
        pore_f = pore[z].astype(jnp.float32)
        wall_f = wall[z].astype(jnp.float32)
        vel = velocity(moments, [left[j, at, :] for j in range(3)], [right[j, at, :] for j in range(3)], pore_f)
        for j in range(3):
            vel_out[j, z] = vel[j]
        first_step(
            z,
            vel,
            pore_f,
            wall_f,
            lambda k: magnet[k, z],
            plus,
            minus,
            lambda k: left[7 + k, at, :],
            lambda k: right[7 + k, at, :],
        )

    halo_layer(low, -1, 1.0)
    own_layer(0, (low, 1.0), lambda k: magnet[k, 1], lambda k: low[7 + k])

    def inner(z, carry):
        own_layer(z, None, lambda k: magnet[k, z + 1], lambda k: magnet[k, z - 1])
        return carry

    lax.fori_loop(1, depth - 1, inner, 0)
    own_layer(depth - 1, (high, -1.0), lambda k: high[7 + k], lambda k: magnet[k, depth - 2])
    halo_layer(high, depth, -1.0)

    def second(z, totals):
        at = pl.ds(z, 1)
        pore_f = pore[z].astype(jnp.float32)
        wall_f = wall[z].astype(jnp.float32)
        coef = coefficients([vel_out[j, z] for j in range(3)], pore_f, wall_f)
        cos, sin = phases(z)
        values = []
        for k in range(4):
            center = mid[k, z + 1]
            y_pair = beside(center, thin[0, k, at, :], thin[1, k, at, :])
            values.append(stencil(coef, center, (mid[k, z + 2], mid[k, z]), y_pair, x_width))
        values = rotate(values, cos, sin)
        for k in range(4):
            mag_out[k, z] = values[k]
        return tuple(t + v for t, v in zip(totals, values))

    zero = jnp.zeros(shape, jnp.float32)
    totals = lax.fori_loop(0, depth, second, (zero, zero, zero, zero))
    sums[...] = jnp.zeros_like(sums)
    for k in range(4):
        line = jnp.sum(totals[k], axis=0, keepdims=True)
        sums[k : k + 1, :] = line[:, :128] + line[:, 128:]


def vmem(count):
    return [pl.BlockSpec(memory_space=pltpu.VMEM)] * count


def struct(*shape):
    return jax.ShapeDtypeStruct(shape, jnp.float32)


def collide(pops, magnet, pore, wall):
    _, depth, width, x_width = pops.shape
    last = depth // 2 - 1
    resident = lambda *shape: pl.BlockSpec(shape, lambda g: (0,) * len(shape))
    return pl.pallas_call(
        collide_kernel,
        grid=(depth // BLOCK,),
        in_specs=[
            pl.BlockSpec((19, BLOCK, width, x_width), lambda g: (0, g, 0, 0)),
            pl.BlockSpec((BLOCK, width, x_width), lambda g: (g, 0, 0)),
            pl.BlockSpec((4, 2, width, x_width), lambda g: (0, 0, 0, 0)),
            pl.BlockSpec((4, 2, width, x_width), lambda g: (0, last, 0, 0)),
            pl.BlockSpec((1, width, x_width), lambda g: (0, 0, 0)),
            pl.BlockSpec((1, width, x_width), lambda g: (depth - 1, 0, 0)),
            pl.BlockSpec((1, width, x_width), lambda g: (0, 0, 0)),
            pl.BlockSpec((1, width, x_width), lambda g: (depth - 1, 0, 0)),
        ],
        out_specs=[
            resident(4, depth + 2, width, x_width),
            resident(2, 4, depth, x_width),
            resident(PLANES, width, x_width),
            resident(PLANES, width, x_width),
        ],
        out_shape=[
            struct(4, depth + 2, width, x_width),
            struct(2, 4, depth, x_width),
            struct(PLANES, width, x_width),
            struct(PLANES, width, x_width),
        ],
        compiler_params=pltpu.CompilerParams(vmem_limit_bytes=VMEM_LIMIT),
        name="collide",
    )(pops, pore, magnet, magnet, pore, pore, wall, wall)


def pack(acc, rows, magnet, pore, wall):
    depth, x_width = rows.shape[2:]
    return pl.pallas_call(
        pack_kernel,
        in_specs=vmem(5),
        out_specs=vmem(2),
        out_shape=[struct(PLANES, depth, x_width)] * 2,
        compiler_params=pltpu.CompilerParams(vmem_limit_bytes=VMEM_LIMIT),
        cost_estimate=pl.CostEstimate(flops=2_000_000, bytes_accessed=6_000_000, transcendentals=0),
        name="pack",
    )(acc, rows, magnet, pore, wall)


def merge(low, high, acc, rows, up, down):
    return pl.pallas_call(
        merge_kernel,
        in_specs=vmem(6),
        out_specs=vmem(2),
        out_shape=[struct(*up.shape)] * 2,
        input_output_aliases={4: 0, 5: 1},
        compiler_params=pltpu.CompilerParams(vmem_limit_bytes=VMEM_LIMIT),
        name="merge",
    )(low, high, acc, rows, up, down)


def finish(table, wide, acc, magnet, pore, wall, low, high, left, right, up, down):
    depth, width, x_width = pore.shape
    return pl.pallas_call(
        final_kernel,
        in_specs=[pl.BlockSpec(memory_space=pltpu.SMEM)] + vmem(11),
        out_specs=vmem(3),
        out_shape=[struct(3, depth, width, x_width), struct(4, depth, width, x_width), struct(8, 128)],
        scratch_shapes=[
            pltpu.VMEM((4, depth + 2, width, x_width), jnp.float32),
            pltpu.VMEM((2, 4, depth, x_width), jnp.float32),
        ],
        compiler_params=pltpu.CompilerParams(vmem_limit_bytes=VMEM_LIMIT),
        name="finish",
    )(table, wide, acc, magnet, pore, wall, low, high, left, right, up, down)


def ring(value, axis, step):
    count = lax.axis_size(axis)
    return lax.ppermute(value, axis, [(i, (i + step) % count) for i in range(count)])


def phase_tables(start, depth, extent):
    layers = jnp.remainder(start + jnp.arange(-1, depth + 1, dtype=jnp.int32), extent)
    coords = layers.astype(jnp.float32)
    wave_numbers = jnp.array([Q_LOW, Q_HIGH], jnp.float32)
    angles = 2.0 * math.pi * wave_numbers[:, None] * coords[None, :] / extent
    return jnp.concatenate([jnp.cos(angles), jnp.sin(angles)], axis=0)


def sum_over(value, axis):
    count = lax.axis_size(axis)
    copies = jnp.broadcast_to(value[None], (count,) + value.shape)
    return jnp.sum(lax.all_to_all(copies, axis, 0, 0), axis=0)


def local(populations, magnetization, pore, wall):
    _, depth, width, x_width = populations.shape
    flow_count = lax.axis_size("flow")
    trans_count = lax.axis_size("trans")
    extent = depth * flow_count
    magnet = magnetization.reshape(4, depth, width, x_width)

    acc, rows, face_up, face_down = collide(populations, magnet, pore, wall)
    low = ring(face_up, "flow", 1)
    high = ring(face_down, "flow", -1)
    up, down = pack(acc, rows, magnet, pore, wall)
    up, down = merge(low, high, acc, rows, up, down)
    left = ring(up, "trans", 1)
    right = ring(down, "trans", -1)

    table = phase_tables(lax.axis_index("flow") * depth, depth, extent)
    wide = jnp.broadcast_to(table[:, 1:-1, None], (4, depth, 128))
    velocity, magnet, sums = finish(table, wide, acc, magnet, pore, wall, low, high, left, right, up, down)

    sums = sum_over(sum_over(sums, "flow"), "trans")
    signal = jnp.sum(sums[:4], axis=1).reshape(2, 2) / math.sqrt(extent * width * trans_count * x_width)
    return (velocity, magnet.reshape(magnetization.shape), signal)


def solution(mesh):
    placed = (
        P(None, "flow", "trans", None),
        P(None, None, "flow", "trans", None),
        P("flow", "trans", None),
        P("flow", "trans", None),
    )
    return jax.shard_map(
        local,
        mesh=mesh,
        in_specs=placed,
        out_specs=(P(None, "flow", "trans", None), P(None, None, "flow", "trans", None), P()),
        check_vma=False,
    )
```

```python
import functools
import math

import jax
import jax.numpy as jnp
from jax import lax
from jax.experimental import pallas as pl
from jax.experimental.pallas import tpu as pltpu
from jax.sharding import PartitionSpec as P

Q_LOW = 2
Q_HIGH = 5
RELAX_TIME = 1.25
BODY_FORCE = 0.002
DIFFUSION = 0.1
SURFACE = 0.4


MIB = 1024 * 1024


def row_mask(shape, row):
    return lax.broadcasted_iota(jnp.int32, shape, 0) == row


def is_even():
    return lax.rem(lax.axis_index("trans"), 2) == 0


def collide_layer(pop, pore):
    p0 = pop(0)
    sums = []
    diffs = []
    for pair in range(9):
        fwd = pop(2 * pair + 1)
        bwd = pop(2 * pair + 2)
        sums.append(fwd + bwd)
        diffs.append(fwd - bwd)
    density = p0
    for s in sums:
        density = density + s
    mom_z = diffs[0] + diffs[3] + diffs[4] + diffs[5] + diffs[6]
    mom_y = diffs[1] + diffs[3] - diffs[4] + diffs[7] + diffs[8]
    mom_x = diffs[2] + diffs[5] - diffs[6] + diffs[7] - diffs[8]
    inv = 1.0 / density
    u_z = mom_z * inv + RELAX_TIME * BODY_FORCE
    u_y = mom_y * inv
    u_x = mom_x * inv
    is_pore = pore > 0
    rate = 1.0 / RELAX_TIME
    keep_s = jnp.where(is_pore, 0.5 * (1.0 - rate), 0.5)
    keep_d = jnp.where(is_pore, 0.5 * (1.0 - rate), -0.5)
    scaled = jnp.where(is_pore, density * (rate / 36.0), 0.0)
    h_z, h_y, h_x = scaled * u_z, scaled * u_y, scaled * u_x
    q_zz, q_yy, q_xx = 4.5 * h_z * u_z, 4.5 * h_y * u_y, 4.5 * h_x * u_x
    base = scaled - (q_zz + q_yy + q_xx) * (1.0 / 3.0)
    m_z, m_y, m_x = 3.0 * h_z, 3.0 * h_y, 3.0 * h_x
    q_zy, q_zx, q_yx = 3.0 * m_z * u_y, 3.0 * m_z * u_x, 3.0 * m_y * u_x
    out = [(keep_s + keep_s) * p0 + 12.0 * base]
    evens = [
        2.0 * (base + q_zz),
        2.0 * (base + q_yy),
        2.0 * (base + q_xx),
    ]
    zy = base + q_zz + q_yy
    zx = base + q_zz + q_xx
    yx = base + q_yy + q_xx
    evens += [zy + q_zy, zy - q_zy, zx + q_zx, zx - q_zx, yx + q_yx, yx - q_yx]
    odds = [2.0 * m_z, 2.0 * m_y, 2.0 * m_x, m_z + m_y, m_z - m_y, m_z + m_x, m_z - m_x, m_y + m_x, m_y - m_x]
    for pair in range(9):
        even = keep_s * sums[pair] + evens[pair]
        odd = keep_d * diffs[pair] + odds[pair]
        out.append(even + odd)
        out.append(even - odd)
    return out


def stream_layer(r):
    width, x_width = r[0].shape
    shape = (width, x_width)
    r = list(r)
    for i, sign in ((5, 1), (11, 1), (14, 1), (15, 1), (18, 1), (6, -1), (12, -1), (13, -1), (16, -1), (17, -1)):
        r[i] = pltpu.roll(r[i], sign % x_width, 1)
    top = row_mask(shape, 0)
    bottom = row_mask(shape, width - 1)
    moved, edges = [], []
    for side, (plain, x_up, x_down, z_up, z_down) in enumerate(((3, 15, 17, 7, 10), (4, 18, 16, 9, 8))):
        both = r[plain] + r[x_up] + r[x_down]
        diff = r[x_up] - r[x_down]
        values = (both, diff, r[z_up], r[z_down])
        edge = width - 1 if side == 0 else 0
        edges.append([v[edge : edge + 1] for v in values])
        turn = 1 if side == 0 else width - 1
        moved.append([jnp.where(top if side == 0 else bottom, 0.0, pltpu.roll(v, turn, 0)) for v in values])
    (up_d, up_x, up_zu, up_zd), (dn_d, dn_x, dn_zu, dn_zd) = moved
    above = (r[1] + r[11] + r[13] + up_zu + dn_zu, up_zu - dn_zu, r[11] - r[13])
    here = (r[0] + r[5] + r[6] + up_d + dn_d, up_d - dn_d, r[5] - r[6] + up_x + dn_x)
    below = (r[2] + r[12] + r[14] + up_zd + dn_zd, up_zd - dn_zd, r[14] - r[12])
    return above, here, below, edges


def edge_kernel(pops, magnet, pore, wall, up, down, near, far, low_p, high_p, mag, por, wal, sems):
    depth, width = por.shape[:2]
    copies = [
        pltpu.make_async_copy(pops.at[:, pl.ds(depth - 2, 2)], high_p, sems.at[0]),
        pltpu.make_async_copy(pops.at[:, pl.ds(0, 2)], low_p, sems.at[1]),
        pltpu.make_async_copy(pore, por, sems.at[2]),
        pltpu.make_async_copy(wall, wal, sems.at[3]),
        pltpu.make_async_copy(magnet, mag, sems.at[4]),
    ]
    for copy in copies:
        copy.start()
    copies[2].wait()
    for face, held, copy, border, behind in ((up, high_p, 0, 1, 0), (down, low_p, 1, 0, 1)):
        copies[copy].wait()
        first = depth - 2 if face is up else 0

        def layer(at):
            return stream_layer(collide_layer(lambda i: held[i, at], por[first + at]))

        above, here, below, edges = layer(border)
        above_in, _, below_in, edges_in = layer(behind)
        cross, along = (above, above_in) if face is up else (below, below_in)
        sign = 1.0 if face is up else -1.0
        for j in range(3):
            face[j] = cross[j]
        face[3] = here[0] + along[0]
        face[4] = sign * along[0]
        face[5] = here[1] + along[1]
        face[6] = here[2] + along[2]
        diag = 2 if face is up else 3
        face[17] = jnp.zeros_like(face[17])
        for side in range(2):
            at = 4 * side
            face[17, at : at + 1, :] = edges[side][diag]
            face[17, at + 1 : at + 2, :] = edges[side][0] + edges_in[side][diag]
            face[17, at + 2 : at + 3, :] = sign * edges_in[side][diag]
            face[17, at + 3 : at + 4, :] = edges[side][1]
    copies[3].wait()
    copies[4].wait()
    for face, border, behind in ((up, depth - 1, depth - 2), (down, 0, 1)):
        face[7:11] = mag[:, border]
        face[11:15] = mag[:, behind]
        face[15] = por[border].astype(jnp.float32)
        face[16] = wal[border].astype(jnp.float32)

    def rows(face, border, behind):
        def layer(z, carry):
            at = pl.ds(z, 1)
            for k in range(4):
                face[k, at, :] = mag[k, z, border : border + 1, :]
                face[4 + k, at, :] = mag[k, z, behind : behind + 1, :]
            face[8, at, :] = por[z, border : border + 1, :].astype(jnp.float32)
            face[9, at, :] = wal[z, border : border + 1, :].astype(jnp.float32)
            return carry

        lax.fori_loop(0, depth, layer, 0, unroll=2)

    even = is_even()

    @pl.when(even)
    def _():
        rows(near, width - 1, width - 2)
        rows(far, 0, 1)

    @pl.when(jnp.logical_not(even))
    def _():
        rows(near, 0, 1)
        rows(far, width - 1, width - 2)


def collide_kernel(pops, pore, acc, up, down, held, por, rows, sems):
    depth, width, x_width = por.shape
    shape = (width, x_width)
    chunks = sems.shape[0] - 1
    size = depth // chunks
    copies = [
        pltpu.make_async_copy(pops.at[:, pl.ds(c * size, size)], held.at[:, pl.ds(c * size, size)], sems.at[c])
        for c in range(chunks)
    ]
    pore_copy = pltpu.make_async_copy(pore, por, sems.at[chunks])
    pore_copy.start()
    for copy in copies:
        copy.start()
    acc[:, 0:2] = jnp.zeros((4, 2) + shape, jnp.float32)

    def layer(z, carry):
        above, here, below, edges = stream_layer(collide_layer(lambda i: held[i, z], por[z]))
        for side in range(2):
            for slot in range(4):
                rows[side, slot, pl.ds(z, 1), :] = edges[side][slot]
        acc[0, z + 2] = above[0]
        acc[1, z + 2] = above[0]
        acc[2, z + 2] = above[1]
        acc[3, z + 2] = above[2]
        acc[0, z + 1] = acc[0, z + 1] + here[0]
        acc[2, z + 1] = acc[2, z + 1] + here[1]
        acc[3, z + 1] = acc[3, z + 1] + here[2]
        acc[0, z] = acc[0, z] + below[0]
        acc[1, z] = acc[1, z] - below[0]
        acc[2, z] = acc[2, z] + below[1]
        acc[3, z] = acc[3, z] + below[2]
        return carry

    pore_copy.wait()
    for c in range(chunks):
        copies[c].wait()
        lax.fori_loop(c * size, (c + 1) * size, layer, 0, unroll=2)

    first = row_mask((depth, x_width), 0)
    final = row_mask((depth, x_width), depth - 1)
    for side, face in ((0, up), (1, down)):
        from_below = jnp.where(first, 0.0, pltpu.roll(rows[side, 2], 1, 0))
        from_above = jnp.where(final, 0.0, pltpu.roll(rows[side, 3], depth - 1, 0))
        face[0] = rows[side, 0] + from_below + from_above
        face[1] = from_below - from_above
        face[2] = rows[side, 1]
        face[7] = jnp.zeros_like(face[7])
        face[7, 0:1, :] = rows[side, 3, 0:1, :]
        face[7, 3:4, :] = rows[side, 2, depth - 1 : depth, :]

    def border(z, carry):
        for face, edge in ((up, width - 1), (down, 0)):
            for k in range(4):
                face[3 + k, pl.ds(z, 1), :] = acc[k, z + 1, edge : edge + 1, :]
        return carry

    lax.fori_loop(0, depth, border, 0, unroll=2)


def merge_kernel(low, high, up, down, near, far):
    depth = up.shape[1]
    width = low.shape[1]

    def put(face, own, side, edge):
        face[...] = own[...]
        at = 4 * side
        for halo, z, sign, base, corner in ((low, 0, 1.0, 0, 6), (high, depth - 1, -1.0, 3, 10)):
            here = slice(z, z + 1)
            diag = halo[17, at : at + 1, :]
            face[0, here, :] = own[0, here, :] + diag
            face[1, here, :] = own[1, here, :] + sign * diag
            cross = halo[0, edge : edge + 1, :]
            face[3, here, :] = own[3, here, :] + cross
            face[4, here, :] = own[4, here, :] + sign * cross
            face[5, here, :] = own[5, here, :] + halo[1, edge : edge + 1, :]
            face[6, here, :] = own[6, here, :] + halo[2, edge : edge + 1, :]
            mine = own[7, base : base + 1, :]
            face[7, base : base + 1, :] = halo[17, at + 1 : at + 2, :] + mine
            face[7, base + 1 : base + 2, :] = halo[17, at + 2 : at + 3, :] - sign * mine
            face[7, base + 2 : base + 3, :] = halo[17, at + 3 : at + 4, :]
            for k in range(4):
                face[7, corner + k : corner + k + 1, :] = halo[7 + k, edge : edge + 1, :]

    even = is_even()

    @pl.when(even)
    def _():
        put(near, up, 0, width - 1)
        put(far, down, 1, 0)

    @pl.when(jnp.logical_not(even))
    def _():
        put(near, down, 1, 0)
        put(far, up, 0, width - 1)


def coefficients(vel, pore, wall):
    half = [0.5 * v for v in vel]
    plain = DIFFUSION * pore
    center = (1.0 - 6.0 * DIFFUSION) * pore - SURFACE * (pore * wall)
    return center, [(plain - h, plain + h) for h in half]


def stencil(coef, center, z_pair, y_pair, x_width):
    mid, ((z_p, z_m), (y_p, y_m), (x_p, x_m)) = coef
    plus_x = pltpu.roll(center, x_width - 1, 1)
    minus_x = pltpu.roll(center, 1, 1)
    return (
        mid * center
        + (z_p * z_pair[0] + z_m * z_pair[1])
        + (y_p * y_pair[0] + y_m * y_pair[1])
        + (x_p * plus_x + x_m * minus_x)
    )


def rotate(values, cos, sin):
    out = []
    for k in range(2):
        re, im = values[2 * k], values[2 * k + 1]
        out.append(re * cos[k] + im * sin[k])
        out.append(im * cos[k] - re * sin[k])
    return out


def beside(center, row_low, row_high):
    width = center.shape[0]
    plus = jnp.where(row_mask(center.shape, width - 1), row_high, pltpu.roll(center, width - 1, 0))
    minus = jnp.where(row_mask(center.shape, 0), row_low, pltpu.roll(center, 1, 0))
    return plus, minus


def phases(table, z):
    return [table[0, z + 1], table[1, z + 1]], [table[2, z + 1], table[3, z + 1]]


def first_kernel(table, magnet, pore, wall, acc, low, high, got_near, got_far, mid, vel, por, wal, mag, sems):
    depth, width, x_width = por.shape
    copies = [
        pltpu.make_async_copy(src, dst, sems.at[i])
        for i, (src, dst) in enumerate(((pore, por), (wall, wal), (magnet, mag)))
    ]
    for copy in copies:
        copy.start()
    for copy in copies:
        copy.wait()
    even = is_even()

    def layer(z, extra, plus, minus):
        moments = [acc[k, z + 1] for k in range(4)]
        if extra is not None:
            halo, sign = extra
            moments = [
                moments[0] + halo[0],
                moments[1] + sign * halo[0],
                moments[2] + halo[1],
                moments[3] + halo[2],
            ]
        pore_f = por[z].astype(jnp.float32)
        scale = pore_f / moments[0]
        speed = [m * scale for m in moments[1:]]
        for j in range(3):
            vel[j, z] = speed[j]
        coef = coefficients(speed, pore_f, wal[z].astype(jnp.float32))
        cos, sin = phases(table, z)
        values = []
        for k in range(4):
            center = mag[k, z]
            row_near = got_near[k, pl.ds(z, 1), :]
            row_far = got_far[k, pl.ds(z, 1), :]
            y_pair = beside(center, jnp.where(even, row_far, row_near), jnp.where(even, row_near, row_far))
            values.append(stencil(coef, center, (plus(k), minus(k)), y_pair, x_width))
        for k, value in enumerate(rotate(values, cos, sin)):
            mid[k, z] = value

    layer(0, (low, 1.0), lambda k: mag[k, 1], lambda k: low[7 + k])

    def inner(z, carry):
        layer(z, None, lambda k: mag[k, z + 1], lambda k: mag[k, z - 1])
        return carry

    lax.fori_loop(1, depth - 1, inner, 0, unroll=2)
    layer(depth - 1, (high, -1.0), lambda k: high[7 + k], lambda k: mag[k, depth - 2])


def second_kernel(
    table, wide, magnet, pore, wall, acc, low, high,
    near_m, far_m, near_w, far_w, got_near_m, got_far_m, got_near_w, got_far_w, mid_in, vel_in,
    vel_out, mag_out, sums, por, wal, inside, mid, vel, new, rows, sides, own, sems,
):
    depth, width, x_width = por.shape
    shape = (width, x_width)
    chunks = 3
    size = depth // chunks
    loads = [
        pltpu.make_async_copy(pore, por, sems.at[0]),
        pltpu.make_async_copy(wall, wal, sems.at[1]),
        pltpu.make_async_copy(magnet.at[:, pl.ds(0, 1)], inside.at[:, pl.ds(0, 1)], sems.at[2]),
        pltpu.make_async_copy(magnet.at[:, pl.ds(depth - 1, 1)], inside.at[:, pl.ds(1, 1)], sems.at[3]),
    ]
    for copy in loads:
        copy.start()
    even = is_even()
    for planes, mine_near, mine_far, near, far in (
        (slice(0, 10), near_m, far_m, got_near_m, got_far_m),
        (slice(10, 18), near_w, far_w, got_near_w, got_far_w),
    ):
        sides[0, planes] = jnp.where(even, far[...], near[...])
        sides[1, planes] = jnp.where(even, near[...], far[...])
        own[0, planes] = jnp.where(even, mine_far[...], mine_near[...])
        own[1, planes] = jnp.where(even, mine_near[...], mine_far[...])

    first = row_mask((depth, x_width), 0)
    final = row_mask((depth, x_width), depth - 1)
    cos = [jnp.concatenate([wide[k], wide[k]], axis=1) for k in range(2)]
    sin = [jnp.concatenate([wide[2 + k], wide[2 + k]], axis=1) for k in range(2)]

    def column(moments, cross, sign, pore_f, wall_f, center, ends, y_pair):
        density = moments(0) + cross(0)
        scale = pore_f / density
        speed = [
            (moments(1) + cross(1)) * scale,
            (moments(2) + sign * cross(0)) * scale,
            (moments(3) + cross(2)) * scale,
        ]
        coef = coefficients(speed, pore_f, wall_f)
        values = []
        for k in range(4):
            low_end, high_end = ends(k)
            mid_k = center(k)
            plus = jnp.where(final, high_end, pltpu.roll(mid_k, depth - 1, 0))
            minus = jnp.where(first, low_end, pltpu.roll(mid_k, 1, 0))
            values.append(stencil(coef, mid_k, (plus, minus), y_pair(k), x_width))
        return speed, rotate(values, cos, sin)

    for side, edge in ((0, 0), (1, width - 1)):
        face, mine = sides.at[side], own.at[side]
        sign = -1.0 if side == 0 else 1.0
        order = (lambda a, b: (a, b)) if side == 0 else (lambda a, b: (b, a))
        _, outer = column(
            lambda j: face[13 + j],
            lambda j: mine[10 + j],
            sign,
            face[8],
            face[9],
            lambda k: face[k],
            lambda k: (face[17, 6 + k : 7 + k, :], face[17, 10 + k : 11 + k, :]),
            lambda k: order(mine[k], face[4 + k]),
        )
        speed, border = column(
            lambda j: mine[13 + j],
            lambda j: face[10 + j],
            -sign,
            mine[8],
            mine[9],
            lambda k: mine[k],
            lambda k: (low[7 + k, edge : edge + 1, :], high[7 + k, edge : edge + 1, :]),
            lambda k: order(mine[4 + k], face[k]),
        )
        for k in range(4):
            rows[side, k] = outer[k]
        for k in range(4):
            rows[side, 4 + k] = border[k]
        for j in range(3):
            rows[side, 8 + j] = speed[j]

    for copy in loads:
        copy.wait()
    top = row_mask(shape, 0)
    bottom = row_mask(shape, width - 1)
    for halo, z, cross, base, corner, inner in ((low, -1, 0, 0, 6, 0), (high, depth, depth + 1, 3, 10, 1)):
        d_l, z_l, x_l = [sides[0, 17, base + j : base + j + 1, :] for j in range(3)]
        d_r, z_r, x_r = [sides[1, 17, base + j : base + j + 1, :] for j in range(3)]
        density = halo[3] + acc[0, cross] + jnp.where(top, d_l, jnp.where(bottom, d_r, 0.0))
        m_z = halo[4] + acc[1, cross] + jnp.where(top, z_l, jnp.where(bottom, z_r, 0.0))
        m_y = halo[5] + acc[2, cross] + jnp.where(top, d_l, jnp.where(bottom, -d_r, 0.0))
        m_x = halo[6] + acc[3, cross] + jnp.where(top, x_l, jnp.where(bottom, x_r, 0.0))
        scale = halo[15] / density
        coef = coefficients([m_z * scale, m_y * scale, m_x * scale], halo[15], halo[16])
        values = []
        for k in range(4):
            center = halo[7 + k]
            z_pair = (inside[k, inner], halo[11 + k])
            z_pair = z_pair if z < 0 else z_pair[::-1]
            at = slice(corner + k, corner + k + 1)
            y_pair = beside(center, sides[0, 17, at, :], sides[1, 17, at, :])
            values.append(stencil(coef, center, z_pair, y_pair, x_width))
        for k, value in enumerate(rotate(values, *phases(table, z))):
            mid[k, z + 1] = value

    def patched(layer, slot, at):
        return jnp.where(top, rows[0, slot, at, :], jnp.where(bottom, rows[1, slot, at, :], layer))

    def second(z, totals, final_layer=False):
        at = pl.ds(z, 1)
        speed = [patched(vel_in[j, z], 8 + j, at) for j in range(3)]
        for j in range(3):
            vel[j, z] = speed[j]
        coef = coefficients(speed, por[z].astype(jnp.float32), wal[z].astype(jnp.float32))
        values = []
        for k in range(4):
            center = mid[k, z + 1]
            if final_layer:
                plus = mid[k, z + 2]
            else:
                plus = patched(mid_in[k, z + 1], 4 + k, pl.ds(z + 1, 1))
                mid[k, z + 2] = plus
            y_pair = beside(center, rows[0, k, at, :], rows[1, k, at, :])
            values.append(stencil(coef, center, (plus, mid[k, z]), y_pair, x_width))
        values = rotate(values, *phases(table, z))
        for k in range(4):
            new[k, z] = values[k]
        return tuple(t + v for t, v in zip(totals, values))

    for k in range(4):
        mid[k, 1] = patched(mid_in[k, 0], 4 + k, pl.ds(0, 1))
    totals = (jnp.zeros(shape, jnp.float32),) * 4
    stores = []
    for c in range(chunks):
        ending = c == chunks - 1
        totals = lax.fori_loop(c * size, (c + 1) * size - (1 if ending else 0), second, totals, unroll=2)
        if ending:
            totals = second(depth - 1, totals, True)
        part = pl.ds(c * size, size)
        stores.append(pltpu.make_async_copy(new.at[:, part], mag_out.at[:, part], sems.at[4 + 2 * c]))
        stores.append(pltpu.make_async_copy(vel.at[:, part], vel_out.at[:, part], sems.at[5 + 2 * c]))
        stores[-2].start()
        stores[-1].start()
    sums[...] = jnp.zeros_like(sums)
    for k in range(4):
        line = jnp.sum(totals[k], axis=0, keepdims=True)
        sums[k : k + 1, :] = line[:, :128] + line[:, 128:]
    for copy in stores:
        copy.wait()


VMEM = pl.BlockSpec(memory_space=pltpu.VMEM)
SMEM = pl.BlockSpec(memory_space=pltpu.SMEM)
HBM = pl.BlockSpec(memory_space=pltpu.HBM)


def struct(*shape):
    return jax.ShapeDtypeStruct(shape, jnp.float32)


def floats(*shape):
    return pltpu.VMEM(shape, jnp.float32)


def ints(*shape):
    return pltpu.VMEM(shape, jnp.int32)


def params(mib):
    return pltpu.CompilerParams(vmem_limit_bytes=mib * MIB)


def edge_faces(pops, magnet, pore, wall):
    depth, width, x_width = pore.shape
    return pl.pallas_call(
        edge_kernel,
        in_specs=[HBM] * 4,
        out_specs=[VMEM] * 4,
        out_shape=[struct(18, width, x_width)] * 2 + [struct(10, depth, x_width)] * 2,
        scratch_shapes=[
            floats(19, 2, width, x_width),
            floats(19, 2, width, x_width),
            floats(4, depth, width, x_width),
            ints(depth, width, x_width),
            ints(depth, width, x_width),
            pltpu.SemaphoreType.DMA((5,)),
        ],
        compiler_params=params(60),
        name="edge_faces",
    )(pops, magnet, pore, wall)


def collide(pops, pore):
    depth, width, x_width = pore.shape
    chunks = 6 if depth % 12 == 0 else 1
    return pl.pallas_call(
        collide_kernel,
        in_specs=[HBM] * 2,
        out_specs=[VMEM] * 3,
        out_shape=[struct(4, depth + 2, width, x_width)] + [struct(8, depth, x_width)] * 2,
        scratch_shapes=[
            floats(19, depth, width, x_width),
            ints(depth, width, x_width),
            floats(2, 4, depth, x_width),
            pltpu.SemaphoreType.DMA((chunks + 1,)),
        ],
        compiler_params=params(48),
        cost_estimate=pl.CostEstimate(flops=20_000_000, bytes_accessed=12_000_000, transcendentals=0),
        name="collide",
    )(pops, pore)


def merge(low, high, up, down):
    return pl.pallas_call(
        merge_kernel,
        in_specs=[VMEM] * 4,
        out_specs=[VMEM] * 2,
        out_shape=[struct(*up.shape)] * 2,
        compiler_params=params(8),
        name="merge",
    )(low, high, up, down)


def first_step(table, magnet, pore, wall, acc, low, high, got_near, got_far):
    depth, width, x_width = pore.shape
    return pl.pallas_call(
        first_kernel,
        in_specs=[SMEM] + [HBM] * 3 + [VMEM] * 5,
        out_specs=[VMEM] * 2,
        out_shape=[struct(4, depth, width, x_width), struct(3, depth, width, x_width)],
        scratch_shapes=[
            ints(depth, width, x_width),
            ints(depth, width, x_width),
            floats(4, depth, width, x_width),
            pltpu.SemaphoreType.DMA((3,)),
        ],
        compiler_params=params(16),
        cost_estimate=pl.CostEstimate(flops=20_000_000, bytes_accessed=6_000_000, transcendentals=0),
        name="first_step",
    )(table, magnet, pore, wall, acc, low, high, got_near, got_far)


def second_step(table, wide, magnet, pore, wall, *rest):
    depth, width, x_width = pore.shape
    return pl.pallas_call(
        second_kernel,
        in_specs=[SMEM, VMEM] + [HBM] * 3 + [VMEM] * len(rest),
        out_specs=[HBM, HBM, VMEM],
        out_shape=[struct(3, depth, width, x_width), struct(4, depth, width, x_width), struct(8, 128)],
        scratch_shapes=[
            ints(depth, width, x_width),
            ints(depth, width, x_width),
            floats(4, 2, width, x_width),
            floats(4, depth + 2, width, x_width),
            floats(3, depth, width, x_width),
            floats(4, depth, width, x_width),
            floats(2, 11, depth, x_width),
            floats(2, 18, depth, x_width),
            floats(2, 18, depth, x_width),
            pltpu.SemaphoreType.DMA((10,)),
        ],
        compiler_params=params(24),
        name="second_step",
    )(table, wide, magnet, pore, wall, *rest)


def ring(value, axis, step):
    count = lax.axis_size(axis)
    return lax.ppermute(value, axis, [(i, (i + step) % count) for i in range(count)])


def swap(value, axis, near):
    count = lax.axis_size(axis)
    step = 1 if near else -1
    return lax.ppermute(value, axis, [(i, (i + (step if i % 2 == 0 else -step)) % count) for i in range(count)])


def phase_tables(start, depth, extent):
    layers = jnp.remainder(start + jnp.arange(-1, depth + 1, dtype=jnp.int32), extent)
    coords = layers.astype(jnp.float32)
    wave_numbers = jnp.array([Q_LOW, Q_HIGH], jnp.float32)
    angles = 2.0 * math.pi * wave_numbers[:, None] * coords[None, :] / extent
    return jnp.concatenate([jnp.cos(angles), jnp.sin(angles)], axis=0)


def sum_over(value, axis):
    count = lax.axis_size(axis)
    copies = jnp.broadcast_to(value[None], (count,) + value.shape)
    return jnp.sum(lax.all_to_all(copies, axis, 0, 0), axis=0)


def local(populations, magnetization, pore, wall):
    _, depth, width, x_width = populations.shape
    flow_count = lax.axis_size("flow")
    trans_count = lax.axis_size("trans")
    extent = depth * flow_count
    magnet = magnetization.reshape(4, depth, width, x_width)
    table = phase_tables(lax.axis_index("flow") * depth, depth, extent)
    wide = jnp.broadcast_to(table[:, 1:-1, None], (4, depth, 128))

    face_up, face_down, near_m, far_m = edge_faces(populations, magnet, pore, wall)
    low = ring(face_up, "flow", 1)
    high = ring(face_down, "flow", -1)
    got_near_m = swap(near_m, "trans", True)
    got_far_m = swap(far_m, "trans", False)
    acc, up, down = collide(populations, pore)
    near_w, far_w = merge(low, high, up, down)
    got_near_w = swap(near_w, "trans", True)
    got_far_w = swap(far_w, "trans", False)
    mid, vel = first_step(table, magnet, pore, wall, acc, low, high, got_near_m, got_far_m)
    velocity, magnet, sums = second_step(
        table, wide, magnet, pore, wall, acc, low, high,
        near_m, far_m, near_w, far_w, got_near_m, got_far_m, got_near_w, got_far_w, mid, vel,
    )
    sums = sum_over(sum_over(sums, "flow"), "trans")
    signal = jnp.sum(sums[:4], axis=1).reshape(2, 2) / math.sqrt(extent * width * trans_count * x_width)
    return (velocity, magnet.reshape(magnetization.shape), signal)


def solution(mesh):
    placed = (
        P(None, "flow", "trans", None),
        P(None, None, "flow", "trans", None),
        P("flow", "trans", None),
        P("flow", "trans", None),
    )
    return jax.shard_map(
        local,
        mesh=mesh,
        in_specs=placed,
        out_specs=(P(None, "flow", "trans", None), P(None, None, "flow", "trans", None), P()),
        check_vma=False,
    )
```

```python
import functools
import math

import jax
import jax.numpy as jnp
from jax import lax
from jax.experimental import pallas as pl
from jax.experimental.pallas import tpu as pltpu
from jax.sharding import PartitionSpec as P

Q_LOW = 2
Q_HIGH = 5
RELAX_TIME = 1.25
BODY_FORCE = 0.002
DIFFUSION = 0.1
SURFACE = 0.4


MIB = 1024 * 1024


def row_mask(shape, row):
    return lax.broadcasted_iota(jnp.int32, shape, 0) == row


def is_even(axis):
    return lax.rem(lax.axis_index(axis), 2) == 0


def collide_layer(pop, pore):
    p0 = pop(0)
    sums = []
    diffs = []
    for pair in range(9):
        fwd = pop(2 * pair + 1)
        bwd = pop(2 * pair + 2)
        sums.append(fwd + bwd)
        diffs.append(fwd - bwd)
    density = p0
    for s in sums:
        density = density + s
    mom_z = diffs[0] + diffs[3] + diffs[4] + diffs[5] + diffs[6]
    mom_y = diffs[1] + diffs[3] - diffs[4] + diffs[7] + diffs[8]
    mom_x = diffs[2] + diffs[5] - diffs[6] + diffs[7] - diffs[8]
    inv = 1.0 / density
    u_z = mom_z * inv + RELAX_TIME * BODY_FORCE
    u_y = mom_y * inv
    u_x = mom_x * inv
    is_pore = pore > 0
    rate = 1.0 / RELAX_TIME
    keep_s = jnp.where(is_pore, 0.5 * (1.0 - rate), 0.5)
    keep_d = jnp.where(is_pore, 0.5 * (1.0 - rate), -0.5)
    scaled = jnp.where(is_pore, density * (rate / 36.0), 0.0)
    h_z, h_y, h_x = scaled * u_z, scaled * u_y, scaled * u_x
    q_zz, q_yy, q_xx = 4.5 * h_z * u_z, 4.5 * h_y * u_y, 4.5 * h_x * u_x
    base = scaled - (q_zz + q_yy + q_xx) * (1.0 / 3.0)
    m_z, m_y, m_x = 3.0 * h_z, 3.0 * h_y, 3.0 * h_x
    q_zy, q_zx, q_yx = 3.0 * m_z * u_y, 3.0 * m_z * u_x, 3.0 * m_y * u_x
    out = [(keep_s + keep_s) * p0 + 12.0 * base]
    evens = [
        2.0 * (base + q_zz),
        2.0 * (base + q_yy),
        2.0 * (base + q_xx),
    ]
    zy = base + q_zz + q_yy
    zx = base + q_zz + q_xx
    yx = base + q_yy + q_xx
    evens += [zy + q_zy, zy - q_zy, zx + q_zx, zx - q_zx, yx + q_yx, yx - q_yx]
    odds = [2.0 * m_z, 2.0 * m_y, 2.0 * m_x, m_z + m_y, m_z - m_y, m_z + m_x, m_z - m_x, m_y + m_x, m_y - m_x]
    for pair in range(9):
        even = keep_s * sums[pair] + evens[pair]
        odd = keep_d * diffs[pair] + odds[pair]
        out.append(even + odd)
        out.append(even - odd)
    return out


def stream_layer(r):
    width, x_width = r[0].shape
    shape = (width, x_width)
    r = list(r)
    for i, sign in ((5, 1), (11, 1), (14, 1), (15, 1), (18, 1), (6, -1), (12, -1), (13, -1), (16, -1), (17, -1)):
        r[i] = pltpu.roll(r[i], sign % x_width, 1)
    top = row_mask(shape, 0)
    bottom = row_mask(shape, width - 1)
    moved, edges = [], []
    for side, (plain, x_up, x_down, z_up, z_down) in enumerate(((3, 15, 17, 7, 10), (4, 18, 16, 9, 8))):
        both = r[plain] + r[x_up] + r[x_down]
        diff = r[x_up] - r[x_down]
        values = (both, diff, r[z_up], r[z_down])
        edge = width - 1 if side == 0 else 0
        edges.append([v[edge : edge + 1] for v in values])
        turn = 1 if side == 0 else width - 1
        moved.append([jnp.where(top if side == 0 else bottom, 0.0, pltpu.roll(v, turn, 0)) for v in values])
    (up_d, up_x, up_zu, up_zd), (dn_d, dn_x, dn_zu, dn_zd) = moved
    above = (r[1] + r[11] + r[13] + up_zu + dn_zu, up_zu - dn_zu, r[11] - r[13])
    here = (r[0] + r[5] + r[6] + up_d + dn_d, up_d - dn_d, r[5] - r[6] + up_x + dn_x)
    below = (r[2] + r[12] + r[14] + up_zd + dn_zd, up_zd - dn_zd, r[14] - r[12])
    return above, here, below, edges


def edge_kernel(
    pops, magnet, pore, wall, z_near, z_far, y_near, y_far, low_p, high_p, mag, por, wal, up, down, left, right, sems
):
    depth, width = por.shape[:2]
    pairs = [
        (pops.at[:, pl.ds(depth - 2, 2)], high_p),
        (pore, por),
        (pops.at[:, pl.ds(0, 2)], low_p),
        (wall, wal),
        (magnet, mag),
    ]
    copies = [pltpu.make_async_copy(src, dst, sems.at[i]) for i, (src, dst) in enumerate(pairs)]
    for copy in copies:
        copy.start()
    copies[1].wait()
    for face, held, copy, border, behind in ((up, high_p, 0, 1, 0), (down, low_p, 2, 0, 1)):
        copies[copy].wait()
        first = depth - 2 if face is up else 0

        def layer(at):
            return stream_layer(collide_layer(lambda i: held[i, at], por[first + at]))

        above, here, below, edges = layer(border)
        above_in, _, below_in, edges_in = layer(behind)
        cross, along = (above, above_in) if face is up else (below, below_in)
        sign = 1.0 if face is up else -1.0
        for j in range(3):
            face[j] = cross[j]
        face[3] = here[0] + along[0]
        face[4] = sign * along[0]
        face[5] = here[1] + along[1]
        face[6] = here[2] + along[2]
        diag = 2 if face is up else 3
        face[17] = jnp.zeros_like(face[17])
        for side in range(2):
            at = 4 * side
            face[17, at : at + 1, :] = edges[side][diag]
            face[17, at + 1 : at + 2, :] = edges[side][0] + edges_in[side][diag]
            face[17, at + 2 : at + 3, :] = sign * edges_in[side][diag]
            face[17, at + 3 : at + 4, :] = edges[side][1]
        if face is up:
            copies[3].wait()
            copies[4].wait()
        at, back = (depth - 1, depth - 2) if face is up else (0, 1)
        face[7:11] = mag[:, at]
        face[11:15] = mag[:, back]
        face[15] = por[at].astype(jnp.float32)
        face[16] = wal[at].astype(jnp.float32)

    def send(even, src, if_even, if_odd, sem):
        to_even = pltpu.make_async_copy(src, if_even, sem)
        to_odd = pltpu.make_async_copy(src, if_odd, sem)

        @pl.when(even)
        def _():
            to_even.start()

        @pl.when(jnp.logical_not(even))
        def _():
            to_odd.start()

        return to_even

    even_z, even_y = is_even("flow"), is_even("trans")
    sent = [
        send(even_z, up, z_near, z_far, sems.at[5]),
        send(even_z, down, z_far, z_near, sems.at[6]),
    ]

    def rows(z, carry):
        at = pl.ds(z, 1)
        for face, border, behind in ((right, width - 1, width - 2), (left, 0, 1)):
            for k in range(4):
                face[k, at, :] = mag[k, z, border : border + 1, :]
                face[4 + k, at, :] = mag[k, z, behind : behind + 1, :]
            face[8, at, :] = por[z, border : border + 1, :].astype(jnp.float32)
            face[9, at, :] = wal[z, border : border + 1, :].astype(jnp.float32)
        return carry

    lax.fori_loop(0, depth, rows, 0, unroll=2)
    sent += [
        send(even_y, right, y_near, y_far, sems.at[7]),
        send(even_y, left, y_far, y_near, sems.at[8]),
    ]
    for copy in sent:
        copy.wait()


def collide_kernel(pops, pore, acc, up, down, held, por, rows, sems):
    depth, width, x_width = por.shape
    shape = (width, x_width)
    chunks = sems.shape[0] - 1
    size = depth // chunks
    copies = [
        pltpu.make_async_copy(pops.at[:, pl.ds(c * size, size)], held.at[:, pl.ds(c * size, size)], sems.at[c])
        for c in range(chunks)
    ]
    pore_copy = pltpu.make_async_copy(pore, por, sems.at[chunks])
    pore_copy.start()
    for copy in copies:
        copy.start()
    acc[:, 0:2] = jnp.zeros((4, 2) + shape, jnp.float32)

    def layer(z, carry):
        above, here, below, edges = stream_layer(collide_layer(lambda i: held[i, z], por[z]))
        for side in range(2):
            for slot in range(4):
                rows[side, slot, pl.ds(z, 1), :] = edges[side][slot]
        acc[0, z + 2] = above[0]
        acc[1, z + 2] = above[0]
        acc[2, z + 2] = above[1]
        acc[3, z + 2] = above[2]
        acc[0, z + 1] = acc[0, z + 1] + here[0]
        acc[2, z + 1] = acc[2, z + 1] + here[1]
        acc[3, z + 1] = acc[3, z + 1] + here[2]
        acc[0, z] = acc[0, z] + below[0]
        acc[1, z] = acc[1, z] - below[0]
        acc[2, z] = acc[2, z] + below[1]
        acc[3, z] = acc[3, z] + below[2]
        return carry

    pore_copy.wait()
    for c in range(chunks):
        copies[c].wait()
        lax.fori_loop(c * size, (c + 1) * size, layer, 0, unroll=2)

    first = row_mask((depth, x_width), 0)
    final = row_mask((depth, x_width), depth - 1)
    for side, face in ((0, up), (1, down)):
        from_below = jnp.where(first, 0.0, pltpu.roll(rows[side, 2], 1, 0))
        from_above = jnp.where(final, 0.0, pltpu.roll(rows[side, 3], depth - 1, 0))
        face[0] = rows[side, 0] + from_below + from_above
        face[1] = from_below - from_above
        face[2] = rows[side, 1]
        face[7] = jnp.zeros_like(face[7])
        face[7, 0:1, :] = rows[side, 3, 0:1, :]
        face[7, 3:4, :] = rows[side, 2, depth - 1 : depth, :]

    def border(z, carry):
        for face, edge in ((up, width - 1), (down, 0)):
            for k in range(4):
                face[3 + k, pl.ds(z, 1), :] = acc[k, z + 1, edge : edge + 1, :]
        return carry

    lax.fori_loop(0, depth, border, 0, unroll=2)


def merge_kernel(got_near, got_far, up, down, near, far, low, high):
    depth = up.shape[1]
    width = low.shape[1]
    even_z = is_even("flow")
    low[...] = jnp.where(even_z, got_far[...], got_near[...])
    high[...] = jnp.where(even_z, got_near[...], got_far[...])

    def put(face, own, side, edge):
        face[...] = own[...]
        at = 4 * side
        for halo, z, sign, base, corner in ((low, 0, 1.0, 0, 6), (high, depth - 1, -1.0, 3, 10)):
            here = slice(z, z + 1)
            diag = halo[17, at : at + 1, :]
            face[0, here, :] = own[0, here, :] + diag
            face[1, here, :] = own[1, here, :] + sign * diag
            cross = halo[0, edge : edge + 1, :]
            face[3, here, :] = own[3, here, :] + cross
            face[4, here, :] = own[4, here, :] + sign * cross
            face[5, here, :] = own[5, here, :] + halo[1, edge : edge + 1, :]
            face[6, here, :] = own[6, here, :] + halo[2, edge : edge + 1, :]
            mine = own[7, base : base + 1, :]
            face[7, base : base + 1, :] = halo[17, at + 1 : at + 2, :] + mine
            face[7, base + 1 : base + 2, :] = halo[17, at + 2 : at + 3, :] - sign * mine
            face[7, base + 2 : base + 3, :] = halo[17, at + 3 : at + 4, :]
            for k in range(4):
                face[7, corner + k : corner + k + 1, :] = halo[7 + k, edge : edge + 1, :]

    even = is_even("trans")

    @pl.when(even)
    def _():
        put(near, up, 0, width - 1)
        put(far, down, 1, 0)

    @pl.when(jnp.logical_not(even))
    def _():
        put(near, down, 1, 0)
        put(far, up, 0, width - 1)


def coefficients(vel, pore, wall):
    half = [0.5 * v for v in vel]
    plain = DIFFUSION * pore
    center = (1.0 - 6.0 * DIFFUSION) * pore - SURFACE * (pore * wall)
    return center, [(plain - h, plain + h) for h in half]


def stencil(coef, center, z_pair, y_pair, x_width):
    mid, ((z_p, z_m), (y_p, y_m), (x_p, x_m)) = coef
    plus_x = pltpu.roll(center, x_width - 1, 1)
    minus_x = pltpu.roll(center, 1, 1)
    return (
        mid * center
        + (z_p * z_pair[0] + z_m * z_pair[1])
        + (y_p * y_pair[0] + y_m * y_pair[1])
        + (x_p * plus_x + x_m * minus_x)
    )


def rotate(values, cos, sin):
    out = []
    for k in range(2):
        re, im = values[2 * k], values[2 * k + 1]
        out.append(re * cos[k] + im * sin[k])
        out.append(im * cos[k] - re * sin[k])
    return out


def beside(center, row_low, row_high):
    width = center.shape[0]
    plus = jnp.where(row_mask(center.shape, width - 1), row_high, pltpu.roll(center, width - 1, 0))
    minus = jnp.where(row_mask(center.shape, 0), row_low, pltpu.roll(center, 1, 0))
    return plus, minus


def phases(table, z):
    return [table[0, z + 1], table[1, z + 1]], [table[2, z + 1], table[3, z + 1]]


def first_kernel(
    table, magnet, pore, wall, acc, low, high, near_m, far_m, near_w, far_w, mid, vel, own, por, wal, mag, sems
):
    depth, width, x_width = por.shape
    copies = [
        pltpu.make_async_copy(src, dst, sems.at[i])
        for i, (src, dst) in enumerate(((pore, por), (wall, wal), (magnet, mag)))
    ]
    for copy in copies:
        copy.start()
    even = is_even("trans")
    for planes, near, far in ((slice(0, 10), near_m, far_m), (slice(10, 18), near_w, far_w)):
        own[0, planes] = jnp.where(even, far[...], near[...])
        own[1, planes] = jnp.where(even, near[...], far[...])
    for copy in copies:
        copy.wait()

    def layer(z, extra, plus, minus):
        moments = [acc[k, z + 1] for k in range(4)]
        if extra is not None:
            halo, sign = extra
            moments = [
                moments[0] + halo[0],
                moments[1] + sign * halo[0],
                moments[2] + halo[1],
                moments[3] + halo[2],
            ]
        pore_f = por[z].astype(jnp.float32)
        scale = pore_f / moments[0]
        speed = [m * scale for m in moments[1:]]
        for j in range(3):
            vel[j, z] = speed[j]
        coef = coefficients(speed, pore_f, wal[z].astype(jnp.float32))
        cos, sin = phases(table, z)
        values = []
        for k in range(4):
            center = mag[k, z]
            y_pair = (pltpu.roll(center, width - 1, 0), pltpu.roll(center, 1, 0))
            values.append(stencil(coef, center, (plus(k), minus(k)), y_pair, x_width))
        for k, value in enumerate(rotate(values, cos, sin)):
            mid[k, z] = value

    layer(0, (low, 1.0), lambda k: mag[k, 1], lambda k: low[7 + k])

    def inner(z, carry):
        layer(z, None, lambda k: mag[k, z + 1], lambda k: mag[k, z - 1])
        return carry

    lax.fori_loop(1, depth - 1, inner, 0, unroll=2)
    layer(depth - 1, (high, -1.0), lambda k: high[7 + k], lambda k: mag[k, depth - 2])


def second_kernel(
    table, wide, magnet, pore, wall, acc, low, high,
    own, got_near_m, got_far_m, got_near, got_far, mid_in, vel_in,
    vel_out, mag_out, sums, por, wal, inside, mid, vel, new, rows, beside_m, beside_w, sems,
):
    depth, width, x_width = por.shape
    shape = (width, x_width)
    chunks = 6 if depth % 6 == 0 else 1
    size = depth // chunks
    loads = [
        pltpu.make_async_copy(pore, por, sems.at[0]),
        pltpu.make_async_copy(wall, wal, sems.at[1]),
        pltpu.make_async_copy(magnet.at[:, pl.ds(0, 1)], inside.at[:, pl.ds(0, 1)], sems.at[2]),
        pltpu.make_async_copy(magnet.at[:, pl.ds(depth - 1, 1)], inside.at[:, pl.ds(1, 1)], sems.at[3]),
    ]
    for copy in loads:
        copy.start()
    even = is_even("trans")
    for pair, near, far in ((beside_m, got_near_m, got_far_m), (beside_w, got_near, got_far)):
        pair[0] = jnp.where(even, far[...], near[...])
        pair[1] = jnp.where(even, near[...], far[...])

    first = row_mask((depth, x_width), 0)
    final = row_mask((depth, x_width), depth - 1)
    cos = [jnp.concatenate([wide[k], wide[k]], axis=1) for k in range(2)]
    sin = [jnp.concatenate([wide[2 + k], wide[2 + k]], axis=1) for k in range(2)]

    def column(moments, cross, sign, pore_f, wall_f, center, ends, y_pair):
        density = moments(0) + cross(0)
        scale = pore_f / density
        speed = [
            (moments(1) + cross(1)) * scale,
            (moments(2) + sign * cross(0)) * scale,
            (moments(3) + cross(2)) * scale,
        ]
        coef = coefficients(speed, pore_f, wall_f)
        values = []
        for k in range(4):
            low_end, high_end = ends(k)
            mid_k = center(k)
            plus = jnp.where(final, high_end, pltpu.roll(mid_k, depth - 1, 0))
            minus = jnp.where(first, low_end, pltpu.roll(mid_k, 1, 0))
            values.append(stencil(coef, mid_k, (plus, minus), y_pair(k), x_width))
        return speed, rotate(values, cos, sin)

    for side, edge in ((0, 0), (1, width - 1)):
        face, mine, late = beside_m.at[side], own.at[side], beside_w.at[side]
        sign = -1.0 if side == 0 else 1.0
        order = (lambda a, b: (a, b)) if side == 0 else (lambda a, b: (b, a))
        _, outer = column(
            lambda j: late[3 + j],
            lambda j: mine[10 + j],
            sign,
            face[8],
            face[9],
            lambda k: face[k],
            lambda k: (late[7, 6 + k : 7 + k, :], late[7, 10 + k : 11 + k, :]),
            lambda k: order(mine[k], face[4 + k]),
        )
        speed, border = column(
            lambda j: mine[13 + j],
            lambda j: late[j],
            -sign,
            mine[8],
            mine[9],
            lambda k: mine[k],
            lambda k: (low[7 + k, edge : edge + 1, :], high[7 + k, edge : edge + 1, :]),
            lambda k: order(mine[4 + k], face[k]),
        )
        for k in range(4):
            rows[side, k] = outer[k]
        for k in range(4):
            rows[side, 4 + k] = border[k]
        for j in range(3):
            rows[side, 8 + j] = speed[j]

    for copy in loads:
        copy.wait()
    top = row_mask(shape, 0)
    bottom = row_mask(shape, width - 1)
    for halo, z, cross, base, corner, inner in ((low, -1, 0, 0, 6, 0), (high, depth, depth + 1, 3, 10, 1)):
        d_l, z_l, x_l = [beside_w[0, 7, base + j : base + j + 1, :] for j in range(3)]
        d_r, z_r, x_r = [beside_w[1, 7, base + j : base + j + 1, :] for j in range(3)]
        density = halo[3] + acc[0, cross] + jnp.where(top, d_l, jnp.where(bottom, d_r, 0.0))
        m_z = halo[4] + acc[1, cross] + jnp.where(top, z_l, jnp.where(bottom, z_r, 0.0))
        m_y = halo[5] + acc[2, cross] + jnp.where(top, d_l, jnp.where(bottom, -d_r, 0.0))
        m_x = halo[6] + acc[3, cross] + jnp.where(top, x_l, jnp.where(bottom, x_r, 0.0))
        scale = halo[15] / density
        coef = coefficients([m_z * scale, m_y * scale, m_x * scale], halo[15], halo[16])
        values = []
        for k in range(4):
            center = halo[7 + k]
            z_pair = (inside[k, inner], halo[11 + k])
            z_pair = z_pair if z < 0 else z_pair[::-1]
            at = slice(corner + k, corner + k + 1)
            y_pair = beside(center, beside_w[0, 7, at, :], beside_w[1, 7, at, :])
            values.append(stencil(coef, center, z_pair, y_pair, x_width))
        for k, value in enumerate(rotate(values, *phases(table, z))):
            mid[k, z + 1] = value

    def patched(layer, slot, at):
        return jnp.where(top, rows[0, slot, at, :], jnp.where(bottom, rows[1, slot, at, :], layer))

    def second(z, totals, final_layer=False):
        at = pl.ds(z, 1)
        speed = [patched(vel_in[j, z], 8 + j, at) for j in range(3)]
        for j in range(3):
            vel[j, z] = speed[j]
        coef = coefficients(speed, por[z].astype(jnp.float32), wal[z].astype(jnp.float32))
        values = []
        for k in range(4):
            center = mid[k, z + 1]
            if final_layer:
                plus = mid[k, z + 2]
            else:
                plus = patched(mid_in[k, z + 1], 4 + k, pl.ds(z + 1, 1))
                mid[k, z + 2] = plus
            y_pair = beside(center, rows[0, k, at, :], rows[1, k, at, :])
            values.append(stencil(coef, center, (plus, mid[k, z]), y_pair, x_width))
        values = rotate(values, *phases(table, z))
        for k in range(4):
            new[k, z] = values[k]
        return tuple(t + v for t, v in zip(totals, values))

    for k in range(4):
        mid[k, 1] = patched(mid_in[k, 0], 4 + k, pl.ds(0, 1))
    totals = (jnp.zeros(shape, jnp.float32),) * 4
    stores = []
    for c in range(chunks):
        ending = c == chunks - 1
        totals = lax.fori_loop(c * size, (c + 1) * size - (1 if ending else 0), second, totals, unroll=2)
        if ending:
            totals = second(depth - 1, totals, True)
        part = pl.ds(c * size, size)
        stores.append(pltpu.make_async_copy(new.at[:, part], mag_out.at[:, part], sems.at[4 + 2 * c]))
        stores.append(pltpu.make_async_copy(vel.at[:, part], vel_out.at[:, part], sems.at[5 + 2 * c]))
        stores[-2].start()
        stores[-1].start()
    lane = lax.broadcasted_iota(jnp.int32, sums.shape, 1)
    row = jnp.zeros(sums.shape, jnp.float32)
    for k in range(4):
        line = jnp.sum(totals[k], axis=0, keepdims=True)
        row = jnp.where(lane == k, jnp.sum(line, axis=1, keepdims=True), row)
    sums[...] = row
    for copy in stores:
        copy.wait()


VMEM = pl.BlockSpec(memory_space=pltpu.VMEM)
SMEM = pl.BlockSpec(memory_space=pltpu.SMEM)
HBM = pl.BlockSpec(memory_space=pltpu.HBM)


def struct(*shape):
    return jax.ShapeDtypeStruct(shape, jnp.float32)


def floats(*shape):
    return pltpu.VMEM(shape, jnp.float32)


def ints(*shape):
    return pltpu.VMEM(shape, jnp.int32)


def params(mib):
    return pltpu.CompilerParams(vmem_limit_bytes=mib * MIB)


def edge_faces(pops, magnet, pore, wall):
    depth, width, x_width = pore.shape
    return pl.pallas_call(
        edge_kernel,
        in_specs=[HBM] * 4,
        out_specs=[HBM] * 4,
        out_shape=[struct(18, width, x_width)] * 2 + [struct(10, depth, x_width)] * 2,
        scratch_shapes=[
            floats(19, 2, width, x_width),
            floats(19, 2, width, x_width),
            floats(4, depth, width, x_width),
            ints(depth, width, x_width),
            ints(depth, width, x_width),
            floats(18, width, x_width),
            floats(18, width, x_width),
            floats(10, depth, x_width),
            floats(10, depth, x_width),
            pltpu.SemaphoreType.DMA((9,)),
        ],
        compiler_params=params(60),
        name="edge_faces",
    )(pops, magnet, pore, wall)


def collide(pops, pore):
    depth, width, x_width = pore.shape
    chunks = 6 if depth % 12 == 0 else 1
    return pl.pallas_call(
        collide_kernel,
        in_specs=[HBM] * 2,
        out_specs=[VMEM] * 3,
        out_shape=[struct(4, depth + 2, width, x_width)] + [struct(8, depth, x_width)] * 2,
        scratch_shapes=[
            floats(19, depth, width, x_width),
            ints(depth, width, x_width),
            floats(2, 4, depth, x_width),
            pltpu.SemaphoreType.DMA((chunks + 1,)),
        ],
        compiler_params=params(48),
        cost_estimate=pl.CostEstimate(flops=20_000_000, bytes_accessed=12_000_000, transcendentals=0),
        name="collide",
    )(pops, pore)


def merge(got_near, got_far, up, down):
    return pl.pallas_call(
        merge_kernel,
        in_specs=[VMEM] * 4,
        out_specs=[VMEM] * 4,
        out_shape=[struct(*up.shape)] * 2 + [struct(*got_near.shape)] * 2,
        compiler_params=params(8),
        name="merge",
    )(got_near, got_far, up, down)


def first_step(table, magnet, pore, wall, acc, low, high, *faces):
    depth, width, x_width = pore.shape
    return pl.pallas_call(
        first_kernel,
        in_specs=[SMEM] + [HBM] * 3 + [VMEM] * (3 + len(faces)),
        out_specs=[VMEM] * 3,
        out_shape=[
            struct(4, depth, width, x_width),
            struct(3, depth, width, x_width),
            struct(2, 18, depth, x_width),
        ],
        scratch_shapes=[
            ints(depth, width, x_width),
            ints(depth, width, x_width),
            floats(4, depth, width, x_width),
            pltpu.SemaphoreType.DMA((3,)),
        ],
        compiler_params=params(16),
        cost_estimate=pl.CostEstimate(flops=20_000_000, bytes_accessed=6_000_000, transcendentals=0),
        name="first_step",
    )(table, magnet, pore, wall, acc, low, high, *faces)


def second_step(table, wide, magnet, pore, wall, *rest):
    depth, width, x_width = pore.shape
    return pl.pallas_call(
        second_kernel,
        in_specs=[SMEM, VMEM] + [HBM] * 3 + [VMEM] * len(rest),
        out_specs=[HBM, HBM, VMEM],
        out_shape=[struct(3, depth, width, x_width), struct(4, depth, width, x_width), struct(1, 128)],
        scratch_shapes=[
            ints(depth, width, x_width),
            ints(depth, width, x_width),
            floats(4, 2, width, x_width),
            floats(4, depth + 2, width, x_width),
            floats(3, depth, width, x_width),
            floats(4, depth, width, x_width),
            floats(2, 11, depth, x_width),
            floats(2, 10, depth, x_width),
            floats(2, 8, depth, x_width),
            pltpu.SemaphoreType.DMA((16,)),
        ],
        compiler_params=params(24),
        name="second_step",
    )(table, wide, magnet, pore, wall, *rest)


def swap(value, axis, near):
    count = lax.axis_size(axis)
    step = 1 if near else -1
    return lax.ppermute(value, axis, [(i, (i + (step if i % 2 == 0 else -step)) % count) for i in range(count)])


def phase_tables(start, depth, extent):
    layers = jnp.remainder(start + jnp.arange(-1, depth + 1, dtype=jnp.int32), extent)
    coords = layers.astype(jnp.float32)
    wave_numbers = jnp.array([Q_LOW, Q_HIGH], jnp.float32)
    angles = 2.0 * math.pi * wave_numbers[:, None] * coords[None, :] / extent
    return jnp.concatenate([jnp.cos(angles), jnp.sin(angles)], axis=0)


def sum_over(value, axes):
    count = math.prod(lax.axis_size(axis) for axis in axes)
    copies = jnp.broadcast_to(value[None], (count,) + value.shape)
    return jnp.sum(lax.all_to_all(copies, axes, 0, 0), axis=(0, 1))


def local(populations, magnetization, pore, wall):
    _, depth, width, x_width = populations.shape
    flow_count = lax.axis_size("flow")
    trans_count = lax.axis_size("trans")
    extent = depth * flow_count
    magnet = magnetization.reshape(4, depth, width, x_width)
    table = phase_tables(lax.axis_index("flow") * depth, depth, extent)
    wide = jnp.broadcast_to(table[:, 1:-1, None], (4, depth, 128))

    near_z, far_z, near_m, far_m = edge_faces(populations, magnet, pore, wall)
    got_near_z = swap(near_z, "flow", True)
    got_far_z = swap(far_z, "flow", False)
    got_near_m = swap(near_m, "trans", True)
    got_far_m = swap(far_m, "trans", False)
    acc, up, down = collide(populations, pore)
    near_w, far_w, low, high = merge(got_near_z, got_far_z, up, down)
    got_near_w = swap(near_w, "trans", True)
    got_far_w = swap(far_w, "trans", False)
    mid, vel, own = first_step(table, magnet, pore, wall, acc, low, high, near_m, far_m, near_w, far_w)
    velocity, magnet, sums = second_step(
        table, wide, magnet, pore, wall, acc, low, high,
        own, got_near_m, got_far_m, got_near_w, got_far_w, mid, vel,
    )
    totals = sum_over(sums, ("flow", "trans"))
    signal = totals[:4].reshape(2, 2) / math.sqrt(extent * width * trans_count * x_width)
    return (velocity, magnet.reshape(magnetization.shape), signal)


def solution(mesh):
    placed = (
        P(None, "flow", "trans", None),
        P(None, None, "flow", "trans", None),
        P("flow", "trans", None),
        P("flow", "trans", None),
    )
    return jax.shard_map(
        local,
        mesh=mesh,
        in_specs=placed,
        out_specs=(P(None, "flow", "trans", None), P(None, None, "flow", "trans", None), P()),
        check_vma=False,
    )
```

```python
import functools
import math

import jax
import jax.numpy as jnp
from jax import lax
from jax.experimental import pallas as pl
from jax.experimental.pallas import tpu as pltpu
from jax.sharding import PartitionSpec as P

Q_LOW = 2
Q_HIGH = 5
RELAX_TIME = 1.25
BODY_FORCE = 0.002
DIFFUSION = 0.1
SURFACE = 0.4


MIB = 1024 * 1024


def row_mask(shape, row):
    return lax.broadcasted_iota(jnp.int32, shape, 0) == row


def is_even(axis):
    return lax.rem(lax.axis_index(axis), 2) == 0


def collide_layer(pop, pore):
    p0 = pop(0)
    sums = []
    diffs = []
    for pair in range(9):
        fwd = pop(2 * pair + 1)
        bwd = pop(2 * pair + 2)
        sums.append(fwd + bwd)
        diffs.append(fwd - bwd)
    density = p0
    for s in sums:
        density = density + s
    mom_z = diffs[0] + diffs[3] + diffs[4] + diffs[5] + diffs[6]
    mom_y = diffs[1] + diffs[3] - diffs[4] + diffs[7] + diffs[8]
    mom_x = diffs[2] + diffs[5] - diffs[6] + diffs[7] - diffs[8]
    inv = 1.0 / density
    u_z = mom_z * inv + RELAX_TIME * BODY_FORCE
    u_y = mom_y * inv
    u_x = mom_x * inv
    is_pore = pore > 0
    rate = 1.0 / RELAX_TIME
    keep_s = jnp.where(is_pore, 0.5 * (1.0 - rate), 0.5)
    keep_d = jnp.where(is_pore, 0.5 * (1.0 - rate), -0.5)
    scaled = jnp.where(is_pore, density * (rate / 36.0), 0.0)
    h_z, h_y, h_x = scaled * u_z, scaled * u_y, scaled * u_x
    q_zz, q_yy, q_xx = 4.5 * h_z * u_z, 4.5 * h_y * u_y, 4.5 * h_x * u_x
    base = scaled - (q_zz + q_yy + q_xx) * (1.0 / 3.0)
    m_z, m_y, m_x = 3.0 * h_z, 3.0 * h_y, 3.0 * h_x
    q_zy, q_zx, q_yx = 3.0 * m_z * u_y, 3.0 * m_z * u_x, 3.0 * m_y * u_x
    out = [(keep_s + keep_s) * p0 + 12.0 * base]
    evens = [
        2.0 * (base + q_zz),
        2.0 * (base + q_yy),
        2.0 * (base + q_xx),
    ]
    zy = base + q_zz + q_yy
    zx = base + q_zz + q_xx
    yx = base + q_yy + q_xx
    evens += [zy + q_zy, zy - q_zy, zx + q_zx, zx - q_zx, yx + q_yx, yx - q_yx]
    odds = [2.0 * m_z, 2.0 * m_y, 2.0 * m_x, m_z + m_y, m_z - m_y, m_z + m_x, m_z - m_x, m_y + m_x, m_y - m_x]
    for pair in range(9):
        even = keep_s * sums[pair] + evens[pair]
        odd = keep_d * diffs[pair] + odds[pair]
        out.append(even + odd)
        out.append(even - odd)
    return out


def stream_layer(r):
    width, x_width = r[0].shape
    shape = (width, x_width)
    r = list(r)
    for i, sign in ((5, 1), (11, 1), (14, 1), (15, 1), (18, 1), (6, -1), (12, -1), (13, -1), (16, -1), (17, -1)):
        r[i] = pltpu.roll(r[i], sign % x_width, 1)
    top = row_mask(shape, 0)
    bottom = row_mask(shape, width - 1)
    moved, edges = [], []
    for side, (plain, x_up, x_down, z_up, z_down) in enumerate(((3, 15, 17, 7, 10), (4, 18, 16, 9, 8))):
        both = r[plain] + r[x_up] + r[x_down]
        diff = r[x_up] - r[x_down]
        values = (both, diff, r[z_up], r[z_down])
        edge = width - 1 if side == 0 else 0
        edges.append([v[edge : edge + 1] for v in values])
        turn = 1 if side == 0 else width - 1
        moved.append([jnp.where(top if side == 0 else bottom, 0.0, pltpu.roll(v, turn, 0)) for v in values])
    (up_d, up_x, up_zu, up_zd), (dn_d, dn_x, dn_zu, dn_zd) = moved
    above = (r[1] + r[11] + r[13] + up_zu + dn_zu, up_zu - dn_zu, r[11] - r[13])
    here = (r[0] + r[5] + r[6] + up_d + dn_d, up_d - dn_d, r[5] - r[6] + up_x + dn_x)
    below = (r[2] + r[12] + r[14] + up_zd + dn_zd, up_zd - dn_zd, r[14] - r[12])
    return above, here, below, edges


def edge_kernel(
    pops, magnet, pore, wall, z_near, z_far, y_near, y_far, low_p, high_p, mag, por, wal, up, down, left, right, sems
):
    depth, width = por.shape[:2]
    pairs = [
        (pops.at[:, pl.ds(depth - 2, 2)], high_p),
        (pore, por),
        (pops.at[:, pl.ds(0, 2)], low_p),
        (wall, wal),
        (magnet, mag),
    ]
    copies = [pltpu.make_async_copy(src, dst, sems.at[i]) for i, (src, dst) in enumerate(pairs)]
    for copy in copies:
        copy.start()
    copies[1].wait()
    for face, held, copy, border, behind in ((up, high_p, 0, 1, 0), (down, low_p, 2, 0, 1)):
        copies[copy].wait()
        first = depth - 2 if face is up else 0

        def layer(at):
            return stream_layer(collide_layer(lambda i: held[i, at], por[first + at]))

        above, here, below, edges = layer(border)
        above_in, _, below_in, edges_in = layer(behind)
        cross, along = (above, above_in) if face is up else (below, below_in)
        sign = 1.0 if face is up else -1.0
        for j in range(3):
            face[j] = cross[j]
        face[3] = here[0] + along[0]
        face[4] = sign * along[0]
        face[5] = here[1] + along[1]
        face[6] = here[2] + along[2]
        diag = 2 if face is up else 3
        face[17] = jnp.zeros_like(face[17])
        for side in range(2):
            at = 4 * side
            face[17, at : at + 1, :] = edges[side][diag]
            face[17, at + 1 : at + 2, :] = edges[side][0] + edges_in[side][diag]
            face[17, at + 2 : at + 3, :] = sign * edges_in[side][diag]
            face[17, at + 3 : at + 4, :] = edges[side][1]
        if face is up:
            copies[3].wait()
            copies[4].wait()
        at, back = (depth - 1, depth - 2) if face is up else (0, 1)
        face[7:11] = mag[:, at]
        face[11:15] = mag[:, back]
        face[15] = por[at].astype(jnp.float32)
        face[16] = wal[at].astype(jnp.float32)

    def send(even, src, if_even, if_odd, sem):
        to_even = pltpu.make_async_copy(src, if_even, sem)
        to_odd = pltpu.make_async_copy(src, if_odd, sem)

        @pl.when(even)
        def _():
            to_even.start()

        @pl.when(jnp.logical_not(even))
        def _():
            to_odd.start()

        return to_even

    even_z, even_y = is_even("flow"), is_even("trans")
    sent = [
        send(even_z, up, z_near, z_far, sems.at[5]),
        send(even_z, down, z_far, z_near, sems.at[6]),
    ]

    def rows(z, carry):
        at = pl.ds(z, 1)
        for face, border, behind in ((right, width - 1, width - 2), (left, 0, 1)):
            for k in range(4):
                face[k, at, :] = mag[k, z, border : border + 1, :]
                face[4 + k, at, :] = mag[k, z, behind : behind + 1, :]
            face[8, at, :] = por[z, border : border + 1, :].astype(jnp.float32)
            face[9, at, :] = wal[z, border : border + 1, :].astype(jnp.float32)
        return carry

    lax.fori_loop(0, depth, rows, 0, unroll=2)
    sent += [
        send(even_y, right, y_near, y_far, sems.at[7]),
        send(even_y, left, y_far, y_near, sems.at[8]),
    ]
    for copy in sent:
        copy.wait()


def collide_kernel(pops, pore, acc, up, down, held, por, rows, sems):
    depth, width, x_width = por.shape
    shape = (width, x_width)
    chunks = sems.shape[0] - 1
    size = depth // chunks
    copies = [
        pltpu.make_async_copy(pops.at[:, pl.ds(c * size, size)], held.at[:, pl.ds(c * size, size)], sems.at[c])
        for c in range(chunks)
    ]
    pore_copy = pltpu.make_async_copy(pore, por, sems.at[chunks])
    pore_copy.start()
    for copy in copies:
        copy.start()
    acc[:, 0:2] = jnp.zeros((4, 2) + shape, jnp.float32)

    def layer(z, carry):
        above, here, below, edges = stream_layer(collide_layer(lambda i: held[i, z], por[z]))
        for side in range(2):
            for slot in range(4):
                rows[side, slot, pl.ds(z, 1), :] = edges[side][slot]
        acc[0, z + 2] = above[0]
        acc[1, z + 2] = above[0]
        acc[2, z + 2] = above[1]
        acc[3, z + 2] = above[2]
        acc[0, z + 1] = acc[0, z + 1] + here[0]
        acc[2, z + 1] = acc[2, z + 1] + here[1]
        acc[3, z + 1] = acc[3, z + 1] + here[2]
        acc[0, z] = acc[0, z] + below[0]
        acc[1, z] = acc[1, z] - below[0]
        acc[2, z] = acc[2, z] + below[1]
        acc[3, z] = acc[3, z] + below[2]
        return carry

    pore_copy.wait()
    for c in range(chunks):
        copies[c].wait()
        lax.fori_loop(c * size, (c + 1) * size, layer, 0, unroll=2)

    first = row_mask((depth, x_width), 0)
    final = row_mask((depth, x_width), depth - 1)
    for side, face in ((0, up), (1, down)):
        from_below = jnp.where(first, 0.0, pltpu.roll(rows[side, 2], 1, 0))
        from_above = jnp.where(final, 0.0, pltpu.roll(rows[side, 3], depth - 1, 0))
        face[0] = rows[side, 0] + from_below + from_above
        face[1] = from_below - from_above
        face[2] = rows[side, 1]
        face[7] = jnp.zeros_like(face[7])
        face[7, 0:1, :] = rows[side, 3, 0:1, :]
        face[7, 3:4, :] = rows[side, 2, depth - 1 : depth, :]

    def border(z, carry):
        for face, edge in ((up, width - 1), (down, 0)):
            for k in range(4):
                face[3 + k, pl.ds(z, 1), :] = acc[k, z + 1, edge : edge + 1, :]
        return carry

    lax.fori_loop(0, depth, border, 0, unroll=2)


def merge_kernel(got_near, got_far, up, down, near, far, low, high):
    depth = up.shape[1]
    width = low.shape[1]
    even_z = is_even("flow")
    low[...] = jnp.where(even_z, got_far[...], got_near[...])
    high[...] = jnp.where(even_z, got_near[...], got_far[...])

    def put(face, own, side, edge):
        face[...] = own[...]
        at = 4 * side
        for halo, z, sign, base, corner in ((low, 0, 1.0, 0, 6), (high, depth - 1, -1.0, 3, 10)):
            here = slice(z, z + 1)
            diag = halo[17, at : at + 1, :]
            face[0, here, :] = own[0, here, :] + diag
            face[1, here, :] = own[1, here, :] + sign * diag
            cross = halo[0, edge : edge + 1, :]
            face[3, here, :] = own[3, here, :] + cross
            face[4, here, :] = own[4, here, :] + sign * cross
            face[5, here, :] = own[5, here, :] + halo[1, edge : edge + 1, :]
            face[6, here, :] = own[6, here, :] + halo[2, edge : edge + 1, :]
            mine = own[7, base : base + 1, :]
            face[7, base : base + 1, :] = halo[17, at + 1 : at + 2, :] + mine
            face[7, base + 1 : base + 2, :] = halo[17, at + 2 : at + 3, :] - sign * mine
            face[7, base + 2 : base + 3, :] = halo[17, at + 3 : at + 4, :]
            for k in range(4):
                face[7, corner + k : corner + k + 1, :] = halo[7 + k, edge : edge + 1, :]

    even = is_even("trans")

    @pl.when(even)
    def _():
        put(near, up, 0, width - 1)
        put(far, down, 1, 0)

    @pl.when(jnp.logical_not(even))
    def _():
        put(near, down, 1, 0)
        put(far, up, 0, width - 1)


def coefficients(vel, pore, wall):
    half = [0.5 * v for v in vel]
    plain = DIFFUSION * pore
    center = (1.0 - 6.0 * DIFFUSION) * pore - SURFACE * (pore * wall)
    return center, [(plain - h, plain + h) for h in half]


def stencil(coef, center, z_pair, y_pair, x_width):
    mid, ((z_p, z_m), (y_p, y_m), (x_p, x_m)) = coef
    plus_x = pltpu.roll(center, x_width - 1, 1)
    minus_x = pltpu.roll(center, 1, 1)
    return (
        mid * center
        + (z_p * z_pair[0] + z_m * z_pair[1])
        + (y_p * y_pair[0] + y_m * y_pair[1])
        + (x_p * plus_x + x_m * minus_x)
    )


def rotate(values, cos, sin):
    out = []
    for k in range(2):
        re, im = values[2 * k], values[2 * k + 1]
        out.append(re * cos[k] + im * sin[k])
        out.append(im * cos[k] - re * sin[k])
    return out


def beside(center, row_low, row_high):
    width = center.shape[0]
    plus = jnp.where(row_mask(center.shape, width - 1), row_high, pltpu.roll(center, width - 1, 0))
    minus = jnp.where(row_mask(center.shape, 0), row_low, pltpu.roll(center, 1, 0))
    return plus, minus


def phases(table, z):
    return [table[0, z + 1], table[1, z + 1]], [table[2, z + 1], table[3, z + 1]]


def turned_pair(center):
    return pltpu.roll(center, center.shape[0] - 1, 0), pltpu.roll(center, 1, 0)


def inner_kernel(
    table, magnet, pore, wall, acc, low, high, near_m, far_m, near_w, far_w,
    vel_out, new_out, own, inner, ends, part, por, wal, mag, mid, vel, new, sems,
):
    depth, width, x_width = por.shape
    copies = [
        pltpu.make_async_copy(src, dst, sems.at[i])
        for i, (src, dst) in enumerate(((pore, por), (wall, wal), (magnet, mag)))
    ]
    for copy in copies:
        copy.start()
    even = is_even("trans")
    for planes, near, far in ((slice(0, 10), near_m, far_m), (slice(10, 18), near_w, far_w)):
        own[0, planes] = jnp.where(even, far[...], near[...])
        own[1, planes] = jnp.where(even, near[...], far[...])
    for copy in copies:
        copy.wait()

    def step(z, speed, pore_f, wall_f, center, plus, minus, put):
        coef = coefficients(speed, pore_f, wall_f)
        values = []
        for k in range(4):
            mid_k = center(k)
            values.append(stencil(coef, mid_k, (plus(k), minus(k)), turned_pair(mid_k), x_width))
        values = rotate(values, *phases(table, z))
        for k in range(4):
            put[k, z + 1 if put is mid else z] = values[k]
        return values

    def layer(z, extra, plus, minus):
        moments = [acc[k, z + 1] for k in range(4)]
        if extra is not None:
            halo, sign = extra
            moments = [
                moments[0] + halo[0],
                moments[1] + sign * halo[0],
                moments[2] + halo[1],
                moments[3] + halo[2],
            ]
        pore_f = por[z].astype(jnp.float32)
        scale = pore_f / moments[0]
        speed = [m * scale for m in moments[1:]]
        for j in range(3):
            vel[j, z] = speed[j]
        step(z, speed, pore_f, wal[z].astype(jnp.float32), lambda k: mag[k, z], plus, minus, mid)

    for halo, z, cross, border in ((low, -1, 0, 0), (high, depth, depth + 1, depth - 1)):
        scale = halo[15] / (halo[3] + acc[0, cross])
        speed = [(halo[4 + j] + acc[1 + j, cross]) * scale for j in range(3)]
        towards, behind = (lambda k: mag[k, border]), (lambda k: halo[11 + k])
        pair = (towards, behind) if z < 0 else (behind, towards)
        step(z, speed, halo[15], halo[16], lambda k: halo[7 + k], *pair, mid)

    layer(0, (low, 1.0), lambda k: mag[k, 1], lambda k: low[7 + k])

    def middle(z, carry):
        layer(z, None, lambda k: mag[k, z + 1], lambda k: mag[k, z - 1])
        return carry

    lax.fori_loop(1, depth - 1, middle, 0, unroll=2)
    layer(depth - 1, (high, -1.0), lambda k: high[7 + k], lambda k: mag[k, depth - 2])

    def second(z, totals):
        speed = [vel[j, z] for j in range(3)]
        pore_f, wall_f = por[z].astype(jnp.float32), wal[z].astype(jnp.float32)
        values = step(
            z, speed, pore_f, wall_f, lambda k: mid[k, z + 1], lambda k: mid[k, z + 2], lambda k: mid[k, z], new
        )
        return tuple(t + v for t, v in zip(totals, values))

    chunks = 6 if depth % 6 == 0 else 1
    size = depth // chunks
    totals = (jnp.zeros((width, x_width), jnp.float32),) * 4
    stores = [pltpu.make_async_copy(vel, vel_out, sems.at[3])]
    stores[0].start()
    for c in range(chunks):
        totals = lax.fori_loop(c * size, (c + 1) * size, second, totals, unroll=2)
        at = pl.ds(c * size, size)
        stores.append(pltpu.make_async_copy(new.at[:, at], new_out.at[:, at], sems.at[4 + c]))
        stores[-1].start()

    def rows(z, carry):
        at = pl.ds(z, 1)
        for side, one, two in ((0, 1, 2), (1, width - 2, width - 3)):
            for k in range(4):
                inner[side, k, at, :] = mid[k, z + 1, one : one + 1, :]
                inner[side, 4 + k, at, :] = mid[k, z + 1, two : two + 1, :]
            for j in range(3):
                inner[side, 8 + j, at, :] = vel[j, z, one : one + 1, :]
            inner[side, 11, at, :] = por[z, one : one + 1, :].astype(jnp.float32)
            inner[side, 12, at, :] = wal[z, one : one + 1, :].astype(jnp.float32)
        return carry

    lax.fori_loop(0, depth, rows, 0, unroll=2)
    line = lax.broadcasted_iota(jnp.int32, (width, x_width), 0)
    kept = jnp.logical_and(line >= 2, line < width - 2)
    part[...] = jnp.zeros_like(part)
    for k in range(4):
        for side, one in ((0, 1), (1, width - 2)):
            ends[side, k : k + 1, :] = mid[k, 0, one : one + 1, :]
            ends[side, 4 + k : 5 + k, :] = mid[k, depth + 1, one : one + 1, :]
        part[k : k + 1, :] = jnp.sum(jnp.where(kept, totals[k], 0.0), axis=0, keepdims=True)
    for copy in stores:
        copy.wait()


def border_kernel(
    table, wide, magnet, acc, low, high, own, inner, ends, part,
    got_near_m, got_far_m, got_near, got_far, vel_in, new_in,
    vel_out, mag_out, sums, inside, beside_m, beside_w, speeds, rows, corners, sems,
):
    depth, x_width = own.shape[2:]
    width = low.shape[1]
    shape = (width, x_width)
    loads = [
        pltpu.make_async_copy(magnet.at[:, pl.ds(0, 1)], inside.at[:, pl.ds(0, 1)], sems.at[0]),
        pltpu.make_async_copy(magnet.at[:, pl.ds(depth - 1, 1)], inside.at[:, pl.ds(1, 1)], sems.at[1]),
    ]
    for copy in loads:
        copy.start()
    even = is_even("trans")
    for pair, near, far in ((beside_m, got_near_m, got_far_m), (beside_w, got_near, got_far)):
        pair[0] = jnp.where(even, far[...], near[...])
        pair[1] = jnp.where(even, near[...], far[...])

    first = row_mask((depth, x_width), 0)
    final = row_mask((depth, x_width), depth - 1)
    cos = [jnp.concatenate([wide[k], wide[k]], axis=1) for k in range(2)]
    sin = [jnp.concatenate([wide[2 + k], wide[2 + k]], axis=1) for k in range(2)]

    def column(speed, pore_f, wall_f, center, end, y_pair):
        coef = coefficients(speed, pore_f, wall_f)
        values = []
        for k in range(4):
            low_end, high_end = end(k)
            mid_k = center(k)
            plus = jnp.where(final, high_end, pltpu.roll(mid_k, depth - 1, 0))
            minus = jnp.where(first, low_end, pltpu.roll(mid_k, 1, 0))
            values.append(stencil(coef, mid_k, (plus, minus), y_pair(k), x_width))
        return rotate(values, cos, sin)

    def flow(moments, cross, sign, pore_f):
        scale = pore_f / (moments(0) + cross(0))
        return [
            (moments(1) + cross(1)) * scale,
            (moments(2) + sign * cross(0)) * scale,
            (moments(3) + cross(2)) * scale,
        ]

    edges = (0, width - 1)
    orders = ((lambda a, b: (a, b)), (lambda a, b: (b, a)))
    stores = []
    for side, edge in enumerate(edges):
        face, mine, late = beside_m.at[side], own.at[side], beside_w.at[side]
        sign = -1.0 if side == 0 else 1.0
        order = orders[side]
        speed = flow(lambda j: late[3 + j], lambda j: mine[10 + j], sign, face[8])
        outer = column(
            speed,
            face[8],
            face[9],
            lambda k: face[k],
            lambda k: (late[7, 6 + k : 7 + k, :], late[7, 10 + k : 11 + k, :]),
            lambda k: order(mine[k], face[4 + k]),
        )
        speed = flow(lambda j: mine[13 + j], lambda j: late[j], -sign, mine[8])
        border = column(
            speed,
            mine[8],
            mine[9],
            lambda k: mine[k],
            lambda k: (low[7 + k, edge : edge + 1, :], high[7 + k, edge : edge + 1, :]),
            lambda k: order(mine[4 + k], face[k]),
        )
        for k in range(4):
            rows[side, 0, k] = outer[k]
            rows[side, 1, k] = border[k]
        for j in range(3):
            speeds[side, j] = speed[j]
        stores.append(pltpu.make_async_copy(speeds.at[side], vel_out.at[:, :, edge], sems.at[2 + side]))
        stores[-1].start()

    for copy in loads:
        copy.wait()
    top = row_mask(shape, 0)
    bottom = row_mask(shape, width - 1)
    for halo, z, cross, base, corner, at_end in ((low, -1, 0, 0, 6, 0), (high, depth, depth + 1, 3, 10, 1)):
        d_l, z_l, x_l = [beside_w[0, 7, base + j : base + j + 1, :] for j in range(3)]
        d_r, z_r, x_r = [beside_w[1, 7, base + j : base + j + 1, :] for j in range(3)]
        density = halo[3] + acc[0, cross] + jnp.where(top, d_l, jnp.where(bottom, d_r, 0.0))
        m_z = halo[4] + acc[1, cross] + jnp.where(top, z_l, jnp.where(bottom, z_r, 0.0))
        m_y = halo[5] + acc[2, cross] + jnp.where(top, d_l, jnp.where(bottom, -d_r, 0.0))
        m_x = halo[6] + acc[3, cross] + jnp.where(top, x_l, jnp.where(bottom, x_r, 0.0))
        scale = halo[15] / density
        coef = coefficients([m_z * scale, m_y * scale, m_x * scale], halo[15], halo[16])
        values = []
        for k in range(4):
            center = halo[7 + k]
            z_pair = (inside[k, at_end], halo[11 + k])
            z_pair = z_pair if z < 0 else z_pair[::-1]
            at = slice(corner + k, corner + k + 1)
            y_pair = beside(center, beside_w[0, 7, at, :], beside_w[1, 7, at, :])
            values.append(stencil(coef, center, z_pair, y_pair, x_width))
        for k, value in enumerate(rotate(values, *phases(table, z))):
            for side, edge in enumerate(edges):
                at = 4 * at_end + k
                corners[side, at : at + 1, :] = value[edge : edge + 1]

    totals = [part[k : k + 1, :] for k in range(4)]
    for side, edge in enumerate(edges):
        mine, own_in, order = own.at[side], inner.at[side], orders[side]
        for row, values in enumerate(
            (
                column(
                    [speeds[side, j] for j in range(3)],
                    mine[8],
                    mine[9],
                    lambda k: rows[side, 1, k],
                    lambda k: (corners[side, k : k + 1, :], corners[side, 4 + k : 5 + k, :]),
                    lambda k: order(own_in[k], rows[side, 0, k]),
                ),
                column(
                    [own_in[8 + j] for j in range(3)],
                    own_in[11],
                    own_in[12],
                    lambda k: own_in[k],
                    lambda k: (ends[side, k : k + 1, :], ends[side, 4 + k : 5 + k, :]),
                    lambda k: order(own_in[4 + k], rows[side, 1, k]),
                ),
            )
        ):
            for k in range(4):
                rows[side, 2 + row, k] = values[k]
                totals[k] = totals[k] + jnp.sum(values[k], axis=0, keepdims=True)
            at = edge + (row if side == 0 else -row)
            stores.append(
                pltpu.make_async_copy(rows.at[side, 2 + row], mag_out.at[:, :, at], sems.at[4 + 2 * side + row])
            )
            stores[-1].start()
    lane = lax.broadcasted_iota(jnp.int32, sums.shape, 1)
    line = jnp.zeros(sums.shape, jnp.float32)
    for k in range(4):
        line = jnp.where(lane == k, jnp.sum(totals[k], axis=1, keepdims=True), line)
    sums[...] = line
    for copy in stores:
        copy.wait()


VMEM = pl.BlockSpec(memory_space=pltpu.VMEM)
SMEM = pl.BlockSpec(memory_space=pltpu.SMEM)
HBM = pl.BlockSpec(memory_space=pltpu.HBM)


def struct(*shape):
    return jax.ShapeDtypeStruct(shape, jnp.float32)


def floats(*shape):
    return pltpu.VMEM(shape, jnp.float32)


def ints(*shape):
    return pltpu.VMEM(shape, jnp.int32)


def params(mib):
    return pltpu.CompilerParams(vmem_limit_bytes=mib * MIB)


def edge_faces(pops, magnet, pore, wall):
    depth, width, x_width = pore.shape
    return pl.pallas_call(
        edge_kernel,
        in_specs=[HBM] * 4,
        out_specs=[HBM] * 4,
        out_shape=[struct(18, width, x_width)] * 2 + [struct(10, depth, x_width)] * 2,
        scratch_shapes=[
            floats(19, 2, width, x_width),
            floats(19, 2, width, x_width),
            floats(4, depth, width, x_width),
            ints(depth, width, x_width),
            ints(depth, width, x_width),
            floats(18, width, x_width),
            floats(18, width, x_width),
            floats(10, depth, x_width),
            floats(10, depth, x_width),
            pltpu.SemaphoreType.DMA((9,)),
        ],
        compiler_params=params(60),
        name="edge_faces",
    )(pops, magnet, pore, wall)


def collide(pops, pore):
    depth, width, x_width = pore.shape
    chunks = 6 if depth % 12 == 0 else 1
    return pl.pallas_call(
        collide_kernel,
        in_specs=[HBM] * 2,
        out_specs=[VMEM] * 3,
        out_shape=[struct(4, depth + 2, width, x_width)] + [struct(8, depth, x_width)] * 2,
        scratch_shapes=[
            floats(19, depth, width, x_width),
            ints(depth, width, x_width),
            floats(2, 4, depth, x_width),
            pltpu.SemaphoreType.DMA((chunks + 1,)),
        ],
        compiler_params=params(48),
        cost_estimate=pl.CostEstimate(flops=20_000_000, bytes_accessed=12_000_000, transcendentals=0),
        name="collide",
    )(pops, pore)


def merge(got_near, got_far, up, down):
    return pl.pallas_call(
        merge_kernel,
        in_specs=[VMEM] * 4,
        out_specs=[VMEM] * 4,
        out_shape=[struct(*up.shape)] * 2 + [struct(*got_near.shape)] * 2,
        compiler_params=params(8),
        name="merge",
    )(got_near, got_far, up, down)


def inner_steps(table, magnet, pore, wall, acc, low, high, *faces):
    depth, width, x_width = pore.shape
    return pl.pallas_call(
        inner_kernel,
        in_specs=[SMEM] + [HBM] * 3 + [VMEM] * (3 + len(faces)),
        out_specs=[HBM] * 2 + [VMEM] * 4,
        out_shape=[
            struct(3, depth, width, x_width),
            struct(4, depth, width, x_width),
            struct(2, 18, depth, x_width),
            struct(2, 13, depth, x_width),
            struct(2, 8, x_width),
            struct(8, x_width),
        ],
        scratch_shapes=[
            ints(depth, width, x_width),
            ints(depth, width, x_width),
            floats(4, depth, width, x_width),
            floats(4, depth + 2, width, x_width),
            floats(3, depth, width, x_width),
            floats(4, depth, width, x_width),
            pltpu.SemaphoreType.DMA((10,)),
        ],
        compiler_params=params(24),
        cost_estimate=pl.CostEstimate(flops=40_000_000, bytes_accessed=9_000_000, transcendentals=0),
        name="inner_steps",
    )(table, magnet, pore, wall, acc, low, high, *faces)


def border_rows(table, wide, magnet, *rest):
    depth, width, x_width = magnet.shape[1:]
    count = len(rest) - 2
    return pl.pallas_call(
        border_kernel,
        in_specs=[SMEM, VMEM, HBM] + [VMEM] * count + [HBM] * 2,
        out_specs=[HBM, HBM, VMEM],
        out_shape=[struct(3, depth, width, x_width), struct(4, depth, width, x_width), struct(1, 128)],
        input_output_aliases={3 + count: 0, 4 + count: 1},
        scratch_shapes=[
            floats(4, 2, width, x_width),
            floats(2, 10, depth, x_width),
            floats(2, 8, depth, x_width),
            floats(2, 3, depth, x_width),
            floats(2, 4, 4, depth, x_width),
            floats(2, 8, x_width),
            pltpu.SemaphoreType.DMA((8,)),
        ],
        compiler_params=params(16),
        name="border_rows",
    )(table, wide, magnet, *rest)


def swap(value, axis, near):
    count = lax.axis_size(axis)
    step = 1 if near else -1
    return lax.ppermute(value, axis, [(i, (i + (step if i % 2 == 0 else -step)) % count) for i in range(count)])


def phase_tables(start, depth, extent):
    layers = jnp.remainder(start + jnp.arange(-1, depth + 1, dtype=jnp.int32), extent)
    coords = layers.astype(jnp.float32)
    wave_numbers = jnp.array([Q_LOW, Q_HIGH], jnp.float32)
    angles = 2.0 * math.pi * wave_numbers[:, None] * coords[None, :] / extent
    return jnp.concatenate([jnp.cos(angles), jnp.sin(angles)], axis=0)


def sum_over(value, axes):
    count = math.prod(lax.axis_size(axis) for axis in axes)
    copies = jnp.broadcast_to(value[None], (count,) + value.shape)
    return jnp.sum(lax.all_to_all(copies, axes, 0, 0), axis=(0, 1))


def local(populations, magnetization, pore, wall):
    _, depth, width, x_width = populations.shape
    flow_count = lax.axis_size("flow")
    trans_count = lax.axis_size("trans")
    extent = depth * flow_count
    magnet = magnetization.reshape(4, depth, width, x_width)
    table = phase_tables(lax.axis_index("flow") * depth, depth, extent)
    wide = jnp.broadcast_to(table[:, 1:-1, None], (4, depth, 128))

    near_z, far_z, near_m, far_m = edge_faces(populations, magnet, pore, wall)
    got_near_z = swap(near_z, "flow", True)
    got_far_z = swap(far_z, "flow", False)
    got_near_m = swap(near_m, "trans", True)
    got_far_m = swap(far_m, "trans", False)
    acc, up, down = collide(populations, pore)
    near_w, far_w, low, high = merge(got_near_z, got_far_z, up, down)
    got_near_w = swap(near_w, "trans", True)
    got_far_w = swap(far_w, "trans", False)
    velocity, magnet_out, own, inner, ends, part = inner_steps(
        table, magnet, pore, wall, acc, low, high, near_m, far_m, near_w, far_w
    )
    velocity, magnet, sums = border_rows(
        table, wide, magnet, acc, low, high, own, inner, ends, part,
        got_near_m, got_far_m, got_near_w, got_far_w, velocity, magnet_out,
    )
    totals = sum_over(sums, ("flow", "trans"))
    signal = totals[:4].reshape(2, 2) / math.sqrt(extent * width * trans_count * x_width)
    return (velocity, magnet.reshape(magnetization.shape), signal)


def solution(mesh):
    placed = (
        P(None, "flow", "trans", None),
        P(None, None, "flow", "trans", None),
        P("flow", "trans", None),
        P("flow", "trans", None),
    )
    return jax.shard_map(
        local,
        mesh=mesh,
        in_specs=placed,
        out_specs=(P(None, "flow", "trans", None), P(None, None, "flow", "trans", None), P()),
        check_vma=False,
    )
```

```python
import functools
import math

import jax
import jax.numpy as jnp
from jax import lax
from jax.experimental import pallas as pl
from jax.experimental.pallas import tpu as pltpu
from jax.sharding import PartitionSpec as P

Q_LOW = 2
Q_HIGH = 5
RELAX_TIME = 1.25
BODY_FORCE = 0.002
DIFFUSION = 0.1
SURFACE = 0.4


MIB = 1024 * 1024


def row_mask(shape, row):
    return lax.broadcasted_iota(jnp.int32, shape, 0) == row


def is_even(axis):
    return lax.rem(lax.axis_index(axis), 2) == 0


def collide_layer(pop, pore):
    p0 = pop(0)
    sums = []
    diffs = []
    for pair in range(9):
        fwd = pop(2 * pair + 1)
        bwd = pop(2 * pair + 2)
        sums.append(fwd + bwd)
        diffs.append(fwd - bwd)
    density = p0
    for s in sums:
        density = density + s
    mom_z = diffs[0] + diffs[3] + diffs[4] + diffs[5] + diffs[6]
    mom_y = diffs[1] + diffs[3] - diffs[4] + diffs[7] + diffs[8]
    mom_x = diffs[2] + diffs[5] - diffs[6] + diffs[7] - diffs[8]
    inv = 1.0 / density
    u_z = mom_z * inv + RELAX_TIME * BODY_FORCE
    u_y = mom_y * inv
    u_x = mom_x * inv
    is_pore = pore > 0
    rate = 1.0 / RELAX_TIME
    keep_s = jnp.where(is_pore, 0.5 * (1.0 - rate), 0.5)
    keep_d = jnp.where(is_pore, 0.5 * (1.0 - rate), -0.5)
    scaled = jnp.where(is_pore, density * (rate / 36.0), 0.0)
    h_z, h_y, h_x = scaled * u_z, scaled * u_y, scaled * u_x
    q_zz, q_yy, q_xx = 4.5 * h_z * u_z, 4.5 * h_y * u_y, 4.5 * h_x * u_x
    base = scaled - (q_zz + q_yy + q_xx) * (1.0 / 3.0)
    m_z, m_y, m_x = 3.0 * h_z, 3.0 * h_y, 3.0 * h_x
    q_zy, q_zx, q_yx = 3.0 * m_z * u_y, 3.0 * m_z * u_x, 3.0 * m_y * u_x
    out = [(keep_s + keep_s) * p0 + 12.0 * base]
    evens = [
        2.0 * (base + q_zz),
        2.0 * (base + q_yy),
        2.0 * (base + q_xx),
    ]
    zy = base + q_zz + q_yy
    zx = base + q_zz + q_xx
    yx = base + q_yy + q_xx
    evens += [zy + q_zy, zy - q_zy, zx + q_zx, zx - q_zx, yx + q_yx, yx - q_yx]
    odds = [2.0 * m_z, 2.0 * m_y, 2.0 * m_x, m_z + m_y, m_z - m_y, m_z + m_x, m_z - m_x, m_y + m_x, m_y - m_x]
    for pair in range(9):
        even = keep_s * sums[pair] + evens[pair]
        odd = keep_d * diffs[pair] + odds[pair]
        out.append(even + odd)
        out.append(even - odd)
    return out


def stream_layer(r):
    width, x_width = r[0].shape
    shape = (width, x_width)
    r = list(r)
    for i, sign in ((5, 1), (11, 1), (14, 1), (15, 1), (18, 1), (6, -1), (12, -1), (13, -1), (16, -1), (17, -1)):
        r[i] = pltpu.roll(r[i], sign % x_width, 1)
    top = row_mask(shape, 0)
    bottom = row_mask(shape, width - 1)
    moved, edges = [], []
    for side, (plain, x_up, x_down, z_up, z_down) in enumerate(((3, 15, 17, 7, 10), (4, 18, 16, 9, 8))):
        both = r[plain] + r[x_up] + r[x_down]
        diff = r[x_up] - r[x_down]
        values = (both, diff, r[z_up], r[z_down])
        edge = width - 1 if side == 0 else 0
        edges.append([v[edge : edge + 1] for v in values])
        turn = 1 if side == 0 else width - 1
        moved.append([jnp.where(top if side == 0 else bottom, 0.0, pltpu.roll(v, turn, 0)) for v in values])
    (up_d, up_x, up_zu, up_zd), (dn_d, dn_x, dn_zu, dn_zd) = moved
    above = (r[1] + r[11] + r[13] + up_zu + dn_zu, up_zu - dn_zu, r[11] - r[13])
    here = (r[0] + r[5] + r[6] + up_d + dn_d, up_d - dn_d, r[5] - r[6] + up_x + dn_x)
    below = (r[2] + r[12] + r[14] + up_zd + dn_zd, up_zd - dn_zd, r[14] - r[12])
    return above, here, below, edges


def edge_kernel(
    pops, magnet, pore, wall, z_near, z_far, y_near, y_far, low_p, high_p, mag, por, wal, up, down, left, right, sems
):
    depth, width = por.shape[:2]
    pairs = [
        (pops.at[:, pl.ds(depth - 2, 2)], high_p),
        (pore, por),
        (pops.at[:, pl.ds(0, 2)], low_p),
        (wall, wal),
        (magnet, mag),
    ]
    copies = [pltpu.make_async_copy(src, dst, sems.at[i]) for i, (src, dst) in enumerate(pairs)]
    for copy in copies:
        copy.start()
    copies[1].wait()
    for face, held, copy, border, behind in ((up, high_p, 0, 1, 0), (down, low_p, 2, 0, 1)):
        copies[copy].wait()
        first = depth - 2 if face is up else 0

        def layer(at):
            return stream_layer(collide_layer(lambda i: held[i, at], por[first + at]))

        above, here, below, edges = layer(border)
        above_in, _, below_in, edges_in = layer(behind)
        cross, along = (above, above_in) if face is up else (below, below_in)
        sign = 1.0 if face is up else -1.0
        for j in range(3):
            face[j] = cross[j]
        face[3] = here[0] + along[0]
        face[4] = sign * along[0]
        face[5] = here[1] + along[1]
        face[6] = here[2] + along[2]
        diag = 2 if face is up else 3
        face[17] = jnp.zeros_like(face[17])
        for side in range(2):
            at = 4 * side
            face[17, at : at + 1, :] = edges[side][diag]
            face[17, at + 1 : at + 2, :] = edges[side][0] + edges_in[side][diag]
            face[17, at + 2 : at + 3, :] = sign * edges_in[side][diag]
            face[17, at + 3 : at + 4, :] = edges[side][1]
        if face is up:
            copies[3].wait()
            copies[4].wait()
        at, back = (depth - 1, depth - 2) if face is up else (0, 1)
        face[7:11] = mag[:, at]
        face[11:15] = mag[:, back]
        face[15] = por[at].astype(jnp.float32)
        face[16] = wal[at].astype(jnp.float32)

    def send(even, src, if_even, if_odd, sem):
        to_even = pltpu.make_async_copy(src, if_even, sem)
        to_odd = pltpu.make_async_copy(src, if_odd, sem)

        @pl.when(even)
        def _():
            to_even.start()

        @pl.when(jnp.logical_not(even))
        def _():
            to_odd.start()

        return to_even

    even_z, even_y = is_even("flow"), is_even("trans")
    sent = [
        send(even_z, up, z_near, z_far, sems.at[5]),
        send(even_z, down, z_far, z_near, sems.at[6]),
    ]

    def rows(z, carry):
        at = pl.ds(z, 1)
        for face, border, behind in ((right, width - 1, width - 2), (left, 0, 1)):
            for k in range(4):
                face[k, at, :] = mag[k, z, border : border + 1, :]
                face[4 + k, at, :] = mag[k, z, behind : behind + 1, :]
            face[8, at, :] = por[z, border : border + 1, :].astype(jnp.float32)
            face[9, at, :] = wal[z, border : border + 1, :].astype(jnp.float32)
        return carry

    lax.fori_loop(0, depth, rows, 0, unroll=6)
    sent += [
        send(even_y, right, y_near, y_far, sems.at[7]),
        send(even_y, left, y_far, y_near, sems.at[8]),
    ]
    for copy in sent:
        copy.wait()


def collide_kernel(pops, pore, acc, up, down, held, por, rows, sems):
    depth, width, x_width = por.shape
    shape = (width, x_width)
    chunks = sems.shape[0] - 1
    size = depth // chunks
    copies = [
        pltpu.make_async_copy(pops.at[:, pl.ds(c * size, size)], held.at[:, pl.ds(c * size, size)], sems.at[c])
        for c in range(chunks)
    ]
    pore_copy = pltpu.make_async_copy(pore, por, sems.at[chunks])
    pore_copy.start()
    for copy in copies:
        copy.start()
    acc[:, 0:2] = jnp.zeros((4, 2) + shape, jnp.float32)

    def layer(z, carry):
        above, here, below, edges = stream_layer(collide_layer(lambda i: held[i, z], por[z]))
        for side in range(2):
            for slot in range(4):
                rows[side, slot, pl.ds(z, 1), :] = edges[side][slot]
        acc[0, z + 2] = above[0]
        acc[1, z + 2] = above[0]
        acc[2, z + 2] = above[1]
        acc[3, z + 2] = above[2]
        acc[0, z + 1] = acc[0, z + 1] + here[0]
        acc[2, z + 1] = acc[2, z + 1] + here[1]
        acc[3, z + 1] = acc[3, z + 1] + here[2]
        acc[0, z] = acc[0, z] + below[0]
        acc[1, z] = acc[1, z] - below[0]
        acc[2, z] = acc[2, z] + below[1]
        acc[3, z] = acc[3, z] + below[2]
        return carry

    pore_copy.wait()
    for c in range(chunks):
        copies[c].wait()
        lax.fori_loop(c * size, (c + 1) * size, layer, 0, unroll=2)

    first = row_mask((depth, x_width), 0)
    final = row_mask((depth, x_width), depth - 1)
    for side, face in ((0, up), (1, down)):
        from_below = jnp.where(first, 0.0, pltpu.roll(rows[side, 2], 1, 0))
        from_above = jnp.where(final, 0.0, pltpu.roll(rows[side, 3], depth - 1, 0))
        face[0] = rows[side, 0] + from_below + from_above
        face[1] = from_below - from_above
        face[2] = rows[side, 1]
        face[7] = jnp.zeros_like(face[7])
        face[7, 0:1, :] = rows[side, 3, 0:1, :]
        face[7, 3:4, :] = rows[side, 2, depth - 1 : depth, :]

    def border(z, carry):
        for face, edge in ((up, width - 1), (down, 0)):
            for k in range(4):
                face[3 + k, pl.ds(z, 1), :] = acc[k, z + 1, edge : edge + 1, :]
        return carry

    lax.fori_loop(0, depth, border, 0, unroll=2)


def merge_kernel(got_near, got_far, up, down, near, far, low, high):
    depth = up.shape[1]
    width = low.shape[1]
    even_z = is_even("flow")
    low[...] = jnp.where(even_z, got_far[...], got_near[...])
    high[...] = jnp.where(even_z, got_near[...], got_far[...])

    def put(face, own, side, edge):
        face[...] = own[...]
        at = 4 * side
        for halo, z, sign, base, corner in ((low, 0, 1.0, 0, 6), (high, depth - 1, -1.0, 3, 10)):
            here = slice(z, z + 1)
            diag = halo[17, at : at + 1, :]
            face[0, here, :] = own[0, here, :] + diag
            face[1, here, :] = own[1, here, :] + sign * diag
            cross = halo[0, edge : edge + 1, :]
            face[3, here, :] = own[3, here, :] + cross
            face[4, here, :] = own[4, here, :] + sign * cross
            face[5, here, :] = own[5, here, :] + halo[1, edge : edge + 1, :]
            face[6, here, :] = own[6, here, :] + halo[2, edge : edge + 1, :]
            mine = own[7, base : base + 1, :]
            face[7, base : base + 1, :] = halo[17, at + 1 : at + 2, :] + mine
            face[7, base + 1 : base + 2, :] = halo[17, at + 2 : at + 3, :] - sign * mine
            face[7, base + 2 : base + 3, :] = halo[17, at + 3 : at + 4, :]
            for k in range(4):
                face[7, corner + k : corner + k + 1, :] = halo[7 + k, edge : edge + 1, :]

    even = is_even("trans")

    @pl.when(even)
    def _():
        put(near, up, 0, width - 1)
        put(far, down, 1, 0)

    @pl.when(jnp.logical_not(even))
    def _():
        put(near, down, 1, 0)
        put(far, up, 0, width - 1)


def coefficients(vel, pore, wall):
    half = [0.5 * v for v in vel]
    plain = DIFFUSION * pore
    center = (1.0 - 6.0 * DIFFUSION) * pore - SURFACE * (pore * wall)
    return center, [(plain - h, plain + h) for h in half]


def stencil(coef, center, z_pair, y_pair, x_width):
    mid, ((z_p, z_m), (y_p, y_m), (x_p, x_m)) = coef
    plus_x = pltpu.roll(center, x_width - 1, 1)
    minus_x = pltpu.roll(center, 1, 1)
    return (
        mid * center
        + (z_p * z_pair[0] + z_m * z_pair[1])
        + (y_p * y_pair[0] + y_m * y_pair[1])
        + (x_p * plus_x + x_m * minus_x)
    )


def rotate(values, cos, sin):
    out = []
    for k in range(2):
        re, im = values[2 * k], values[2 * k + 1]
        out.append(re * cos[k] + im * sin[k])
        out.append(im * cos[k] - re * sin[k])
    return out


def beside(center, row_low, row_high):
    width = center.shape[0]
    plus = jnp.where(row_mask(center.shape, width - 1), row_high, pltpu.roll(center, width - 1, 0))
    minus = jnp.where(row_mask(center.shape, 0), row_low, pltpu.roll(center, 1, 0))
    return plus, minus


def phases(table, z):
    return [table[0, z + 1], table[1, z + 1]], [table[2, z + 1], table[3, z + 1]]


def turned_pair(center):
    return pltpu.roll(center, center.shape[0] - 1, 0), pltpu.roll(center, 1, 0)


def inner_kernel(
    table, magnet, pore, wall, acc, low, high, near_m, far_m, near_w, far_w,
    vel_out, new_out, own, inner, ends, part, por, wal, mag, mid, vel, new, sems,
):
    depth, width, x_width = por.shape
    copies = [
        pltpu.make_async_copy(src, dst, sems.at[i])
        for i, (src, dst) in enumerate(((pore, por), (wall, wal), (magnet, mag)))
    ]
    for copy in copies:
        copy.start()
    even = is_even("trans")
    for planes, near, far in ((slice(0, 10), near_m, far_m), (slice(10, 18), near_w, far_w)):
        own[0, planes] = jnp.where(even, far[...], near[...])
        own[1, planes] = jnp.where(even, near[...], far[...])
    for copy in copies:
        copy.wait()

    def step(z, speed, pore_f, wall_f, center, plus, minus, put):
        coef = coefficients(speed, pore_f, wall_f)
        values = []
        for k in range(4):
            mid_k = center(k)
            values.append(stencil(coef, mid_k, (plus(k), minus(k)), turned_pair(mid_k), x_width))
        values = rotate(values, *phases(table, z))
        for k in range(4):
            put[k, z + 1 if put is mid else z] = values[k]
        return values

    def layer(z, extra, plus, minus):
        moments = [acc[k, z + 1] for k in range(4)]
        if extra is not None:
            halo, sign = extra
            moments = [
                moments[0] + halo[0],
                moments[1] + sign * halo[0],
                moments[2] + halo[1],
                moments[3] + halo[2],
            ]
        pore_f = por[z].astype(jnp.float32)
        scale = pore_f / moments[0]
        speed = [m * scale for m in moments[1:]]
        for j in range(3):
            vel[j, z] = speed[j]
        step(z, speed, pore_f, wal[z].astype(jnp.float32), lambda k: mag[k, z], plus, minus, mid)

    for halo, z, cross, border in ((low, -1, 0, 0), (high, depth, depth + 1, depth - 1)):
        scale = halo[15] / (halo[3] + acc[0, cross])
        speed = [(halo[4 + j] + acc[1 + j, cross]) * scale for j in range(3)]
        towards, behind = (lambda k: mag[k, border]), (lambda k: halo[11 + k])
        pair = (towards, behind) if z < 0 else (behind, towards)
        step(z, speed, halo[15], halo[16], lambda k: halo[7 + k], *pair, mid)

    layer(0, (low, 1.0), lambda k: mag[k, 1], lambda k: low[7 + k])

    def middle(z, carry):
        layer(z, None, lambda k: mag[k, z + 1], lambda k: mag[k, z - 1])
        return carry

    lax.fori_loop(1, depth - 1, middle, 0, unroll=2)
    layer(depth - 1, (high, -1.0), lambda k: high[7 + k], lambda k: mag[k, depth - 2])

    def second(z, totals):
        speed = [vel[j, z] for j in range(3)]
        pore_f, wall_f = por[z].astype(jnp.float32), wal[z].astype(jnp.float32)
        values = step(
            z, speed, pore_f, wall_f, lambda k: mid[k, z + 1], lambda k: mid[k, z + 2], lambda k: mid[k, z], new
        )
        return tuple(t + v for t, v in zip(totals, values))

    chunks = 6 if depth % 6 == 0 else 1
    size = depth // chunks
    totals = (jnp.zeros((width, x_width), jnp.float32),) * 4
    stores = [pltpu.make_async_copy(vel, vel_out, sems.at[3])]
    stores[0].start()
    for c in range(chunks):
        totals = lax.fori_loop(c * size, (c + 1) * size, second, totals, unroll=2)
        at = pl.ds(c * size, size)
        stores.append(pltpu.make_async_copy(new.at[:, at], new_out.at[:, at], sems.at[4 + c]))
        stores[-1].start()

    def rows(z, carry):
        at = pl.ds(z, 1)
        for side, one, two in ((0, 1, 2), (1, width - 2, width - 3)):
            for k in range(4):
                inner[side, k, at, :] = mid[k, z + 1, one : one + 1, :]
                inner[side, 4 + k, at, :] = mid[k, z + 1, two : two + 1, :]
            for j in range(3):
                inner[side, 8 + j, at, :] = vel[j, z, one : one + 1, :]
            inner[side, 11, at, :] = por[z, one : one + 1, :].astype(jnp.float32)
            inner[side, 12, at, :] = wal[z, one : one + 1, :].astype(jnp.float32)
        return carry

    lax.fori_loop(0, depth, rows, 0, unroll=2)
    line = lax.broadcasted_iota(jnp.int32, (width, x_width), 0)
    kept = jnp.logical_and(line >= 2, line < width - 2)
    part[...] = jnp.zeros_like(part)
    for k in range(4):
        for side, one in ((0, 1), (1, width - 2)):
            ends[side, k : k + 1, :] = mid[k, 0, one : one + 1, :]
            ends[side, 4 + k : 5 + k, :] = mid[k, depth + 1, one : one + 1, :]
        part[k : k + 1, :] = jnp.sum(jnp.where(kept, totals[k], 0.0), axis=0, keepdims=True)
    for copy in stores:
        copy.wait()


def border_kernel(
    table, wide, magnet, acc, low, high, own, inner, ends, part,
    got_near_m, got_far_m, got_near, got_far, vel_in, new_in,
    vel_out, mag_out, sums, inside, beside_m, beside_w, speeds, rows, corners, sems,
):
    depth, x_width = own.shape[2:]
    width = low.shape[1]
    shape = (width, x_width)
    loads = [
        pltpu.make_async_copy(magnet.at[:, pl.ds(0, 1)], inside.at[:, pl.ds(0, 1)], sems.at[0]),
        pltpu.make_async_copy(magnet.at[:, pl.ds(depth - 1, 1)], inside.at[:, pl.ds(1, 1)], sems.at[1]),
    ]
    for copy in loads:
        copy.start()
    even = is_even("trans")
    for pair, near, far in ((beside_m, got_near_m, got_far_m), (beside_w, got_near, got_far)):
        pair[0] = jnp.where(even, far[...], near[...])
        pair[1] = jnp.where(even, near[...], far[...])

    first = row_mask((depth, x_width), 0)
    final = row_mask((depth, x_width), depth - 1)
    cos = [jnp.concatenate([wide[k], wide[k]], axis=1) for k in range(2)]
    sin = [jnp.concatenate([wide[2 + k], wide[2 + k]], axis=1) for k in range(2)]

    def column(speed, pore_f, wall_f, center, end, y_pair):
        coef = coefficients(speed, pore_f, wall_f)
        values = []
        for k in range(4):
            low_end, high_end = end(k)
            mid_k = center(k)
            plus = jnp.where(final, high_end, pltpu.roll(mid_k, depth - 1, 0))
            minus = jnp.where(first, low_end, pltpu.roll(mid_k, 1, 0))
            values.append(stencil(coef, mid_k, (plus, minus), y_pair(k), x_width))
        return rotate(values, cos, sin)

    def flow(moments, cross, sign, pore_f):
        scale = pore_f / (moments(0) + cross(0))
        return [
            (moments(1) + cross(1)) * scale,
            (moments(2) + sign * cross(0)) * scale,
            (moments(3) + cross(2)) * scale,
        ]

    edges = (0, width - 1)
    orders = ((lambda a, b: (a, b)), (lambda a, b: (b, a)))
    stores = []
    for side, edge in enumerate(edges):
        face, mine, late = beside_m.at[side], own.at[side], beside_w.at[side]
        sign = -1.0 if side == 0 else 1.0
        order = orders[side]
        speed = flow(lambda j: late[3 + j], lambda j: mine[10 + j], sign, face[8])
        outer = column(
            speed,
            face[8],
            face[9],
            lambda k: face[k],
            lambda k: (late[7, 6 + k : 7 + k, :], late[7, 10 + k : 11 + k, :]),
            lambda k: order(mine[k], face[4 + k]),
        )
        speed = flow(lambda j: mine[13 + j], lambda j: late[j], -sign, mine[8])
        border = column(
            speed,
            mine[8],
            mine[9],
            lambda k: mine[k],
            lambda k: (low[7 + k, edge : edge + 1, :], high[7 + k, edge : edge + 1, :]),
            lambda k: order(mine[4 + k], face[k]),
        )
        for k in range(4):
            rows[side, 0, k] = outer[k]
            rows[side, 1, k] = border[k]
        for j in range(3):
            speeds[side, j] = speed[j]
        stores.append(pltpu.make_async_copy(speeds.at[side], vel_out.at[:, :, edge], sems.at[2 + side]))
        stores[-1].start()

    for copy in loads:
        copy.wait()
    top = row_mask(shape, 0)
    bottom = row_mask(shape, width - 1)
    for halo, z, cross, base, corner, at_end in ((low, -1, 0, 0, 6, 0), (high, depth, depth + 1, 3, 10, 1)):
        d_l, z_l, x_l = [beside_w[0, 7, base + j : base + j + 1, :] for j in range(3)]
        d_r, z_r, x_r = [beside_w[1, 7, base + j : base + j + 1, :] for j in range(3)]
        density = halo[3] + acc[0, cross] + jnp.where(top, d_l, jnp.where(bottom, d_r, 0.0))
        m_z = halo[4] + acc[1, cross] + jnp.where(top, z_l, jnp.where(bottom, z_r, 0.0))
        m_y = halo[5] + acc[2, cross] + jnp.where(top, d_l, jnp.where(bottom, -d_r, 0.0))
        m_x = halo[6] + acc[3, cross] + jnp.where(top, x_l, jnp.where(bottom, x_r, 0.0))
        scale = halo[15] / density
        coef = coefficients([m_z * scale, m_y * scale, m_x * scale], halo[15], halo[16])
        values = []
        for k in range(4):
            center = halo[7 + k]
            z_pair = (inside[k, at_end], halo[11 + k])
            z_pair = z_pair if z < 0 else z_pair[::-1]
            at = slice(corner + k, corner + k + 1)
            y_pair = beside(center, beside_w[0, 7, at, :], beside_w[1, 7, at, :])
            values.append(stencil(coef, center, z_pair, y_pair, x_width))
        for k, value in enumerate(rotate(values, *phases(table, z))):
            for side, edge in enumerate(edges):
                at = 4 * at_end + k
                corners[side, at : at + 1, :] = value[edge : edge + 1]

    totals = [part[k : k + 1, :] for k in range(4)]
    for side, edge in enumerate(edges):
        mine, own_in, order = own.at[side], inner.at[side], orders[side]
        for row, values in enumerate(
            (
                column(
                    [speeds[side, j] for j in range(3)],
                    mine[8],
                    mine[9],
                    lambda k: rows[side, 1, k],
                    lambda k: (corners[side, k : k + 1, :], corners[side, 4 + k : 5 + k, :]),
                    lambda k: order(own_in[k], rows[side, 0, k]),
                ),
                column(
                    [own_in[8 + j] for j in range(3)],
                    own_in[11],
                    own_in[12],
                    lambda k: own_in[k],
                    lambda k: (ends[side, k : k + 1, :], ends[side, 4 + k : 5 + k, :]),
                    lambda k: order(own_in[4 + k], rows[side, 1, k]),
                ),
            )
        ):
            for k in range(4):
                rows[side, 2 + row, k] = values[k]
                totals[k] = totals[k] + jnp.sum(values[k], axis=0, keepdims=True)
            at = edge + (row if side == 0 else -row)
            stores.append(
                pltpu.make_async_copy(rows.at[side, 2 + row], mag_out.at[:, :, at], sems.at[4 + 2 * side + row])
            )
            stores[-1].start()
    lane = lax.broadcasted_iota(jnp.int32, sums.shape, 1)
    line = jnp.zeros(sums.shape, jnp.float32)
    for k in range(4):
        line = jnp.where(lane == k, jnp.sum(totals[k], axis=1, keepdims=True), line)
    sums[...] = line
    for copy in stores:
        copy.wait()


VMEM = pl.BlockSpec(memory_space=pltpu.VMEM)
SMEM = pl.BlockSpec(memory_space=pltpu.SMEM)
HBM = pl.BlockSpec(memory_space=pltpu.HBM)


def struct(*shape):
    return jax.ShapeDtypeStruct(shape, jnp.float32)


def floats(*shape):
    return pltpu.VMEM(shape, jnp.float32)


def ints(*shape):
    return pltpu.VMEM(shape, jnp.int32)


def params(mib):
    return pltpu.CompilerParams(vmem_limit_bytes=mib * MIB)


def edge_faces(pops, magnet, pore, wall):
    depth, width, x_width = pore.shape
    return pl.pallas_call(
        edge_kernel,
        in_specs=[HBM] * 4,
        out_specs=[HBM] * 4,
        out_shape=[struct(18, width, x_width)] * 2 + [struct(10, depth, x_width)] * 2,
        scratch_shapes=[
            floats(19, 2, width, x_width),
            floats(19, 2, width, x_width),
            floats(4, depth, width, x_width),
            ints(depth, width, x_width),
            ints(depth, width, x_width),
            floats(18, width, x_width),
            floats(18, width, x_width),
            floats(10, depth, x_width),
            floats(10, depth, x_width),
            pltpu.SemaphoreType.DMA((9,)),
        ],
        compiler_params=params(60),
        name="edge_faces",
    )(pops, magnet, pore, wall)


def collide(pops, pore):
    depth, width, x_width = pore.shape
    chunks = 12 if depth % 24 == 0 else 1
    return pl.pallas_call(
        collide_kernel,
        in_specs=[HBM] * 2,
        out_specs=[VMEM] * 3,
        out_shape=[struct(4, depth + 2, width, x_width)] + [struct(8, depth, x_width)] * 2,
        scratch_shapes=[
            floats(19, depth, width, x_width),
            ints(depth, width, x_width),
            floats(2, 4, depth, x_width),
            pltpu.SemaphoreType.DMA((chunks + 1,)),
        ],
        compiler_params=params(48),
        cost_estimate=pl.CostEstimate(flops=20_000_000, bytes_accessed=12_000_000, transcendentals=0),
        name="collide",
    )(pops, pore)


def merge(got_near, got_far, up, down):
    return pl.pallas_call(
        merge_kernel,
        in_specs=[VMEM] * 4,
        out_specs=[VMEM] * 4,
        out_shape=[struct(*up.shape)] * 2 + [struct(*got_near.shape)] * 2,
        compiler_params=params(8),
        name="merge",
    )(got_near, got_far, up, down)


def inner_steps(table, magnet, pore, wall, acc, low, high, *faces):
    depth, width, x_width = pore.shape
    return pl.pallas_call(
        inner_kernel,
        in_specs=[SMEM] + [HBM] * 3 + [VMEM] * (3 + len(faces)),
        out_specs=[HBM] * 2 + [VMEM] * 4,
        out_shape=[
            struct(3, depth, width, x_width),
            struct(4, depth, width, x_width),
            struct(2, 18, depth, x_width),
            struct(2, 13, depth, x_width),
            struct(2, 8, x_width),
            struct(8, x_width),
        ],
        scratch_shapes=[
            ints(depth, width, x_width),
            ints(depth, width, x_width),
            floats(4, depth, width, x_width),
            floats(4, depth + 2, width, x_width),
            floats(3, depth, width, x_width),
            floats(4, depth, width, x_width),
            pltpu.SemaphoreType.DMA((10,)),
        ],
        compiler_params=params(24),
        cost_estimate=pl.CostEstimate(flops=40_000_000, bytes_accessed=9_000_000, transcendentals=0),
        name="inner_steps",
    )(table, magnet, pore, wall, acc, low, high, *faces)


def border_rows(table, wide, magnet, *rest):
    depth, width, x_width = magnet.shape[1:]
    count = len(rest) - 2
    return pl.pallas_call(
        border_kernel,
        in_specs=[SMEM, VMEM, HBM] + [VMEM] * count + [HBM] * 2,
        out_specs=[HBM, HBM, VMEM],
        out_shape=[struct(3, depth, width, x_width), struct(4, depth, width, x_width), struct(1, 128)],
        input_output_aliases={3 + count: 0, 4 + count: 1},
        scratch_shapes=[
            floats(4, 2, width, x_width),
            floats(2, 10, depth, x_width),
            floats(2, 8, depth, x_width),
            floats(2, 3, depth, x_width),
            floats(2, 4, 4, depth, x_width),
            floats(2, 8, x_width),
            pltpu.SemaphoreType.DMA((8,)),
        ],
        compiler_params=params(16),
        name="border_rows",
    )(table, wide, magnet, *rest)


def swap(value, axis, near):
    count = lax.axis_size(axis)
    step = 1 if near else -1
    return lax.ppermute(value, axis, [(i, (i + (step if i % 2 == 0 else -step)) % count) for i in range(count)])


def phase_tables(start, depth, extent):
    layers = jnp.remainder(start + jnp.arange(-1, depth + 1, dtype=jnp.int32), extent)
    coords = layers.astype(jnp.float32)
    wave_numbers = jnp.array([Q_LOW, Q_HIGH], jnp.float32)
    angles = 2.0 * math.pi * wave_numbers[:, None] * coords[None, :] / extent
    return jnp.concatenate([jnp.cos(angles), jnp.sin(angles)], axis=0)


def sum_over(value, axes):
    count = math.prod(lax.axis_size(axis) for axis in axes)
    copies = jnp.broadcast_to(value[None], (count,) + value.shape)
    return jnp.sum(lax.all_to_all(copies, axes, 0, 0), axis=(0, 1))


def local(populations, magnetization, pore, wall):
    _, depth, width, x_width = populations.shape
    flow_count = lax.axis_size("flow")
    trans_count = lax.axis_size("trans")
    extent = depth * flow_count
    magnet = magnetization.reshape(4, depth, width, x_width)
    table = phase_tables(lax.axis_index("flow") * depth, depth, extent)
    wide = jnp.broadcast_to(table[:, 1:-1, None], (4, depth, 128))

    near_z, far_z, near_m, far_m = edge_faces(populations, magnet, pore, wall)
    near_m, table, wide = lax.optimization_barrier((near_m, table, wide))
    got_near_z = swap(near_z, "flow", True)
    got_far_z = swap(far_z, "flow", False)
    got_near_m = swap(near_m, "trans", True)
    got_far_m = swap(far_m, "trans", False)
    acc, up, down = collide(populations, pore)
    near_w, far_w, low, high = merge(got_near_z, got_far_z, up, down)
    got_near_w = swap(near_w, "trans", True)
    got_far_w = swap(far_w, "trans", False)
    velocity, magnet_out, own, inner, ends, part = inner_steps(
        table, magnet, pore, wall, acc, low, high, near_m, far_m, near_w, far_w
    )
    velocity, magnet, sums = border_rows(
        table, wide, magnet, acc, low, high, own, inner, ends, part,
        got_near_m, got_far_m, got_near_w, got_far_w, velocity, magnet_out,
    )
    totals = sum_over(sums, ("flow", "trans"))
    signal = totals[:4].reshape(2, 2) / math.sqrt(extent * width * trans_count * x_width)
    return (velocity, magnet.reshape(magnetization.shape), signal)


def solution(mesh):
    placed = (
        P(None, "flow", "trans", None),
        P(None, None, "flow", "trans", None),
        P("flow", "trans", None),
        P("flow", "trans", None),
    )
    return jax.shard_map(
        local,
        mesh=mesh,
        in_specs=placed,
        out_specs=(P(None, "flow", "trans", None), P(None, None, "flow", "trans", None), P()),
        check_vma=False,
    )
```

```python
import functools
import math

import jax
import jax.numpy as jnp
from jax import lax
from jax.experimental import pallas as pl
from jax.experimental.pallas import tpu as pltpu
from jax.sharding import PartitionSpec as P

Q_LOW = 2
Q_HIGH = 5
RELAX_TIME = 1.25
BODY_FORCE = 0.002
DIFFUSION = 0.1
SURFACE = 0.4


MIB = 1024 * 1024


def row_mask(shape, row):
    return lax.broadcasted_iota(jnp.int32, shape, 0) == row


def is_even(axis):
    return lax.rem(lax.axis_index(axis), 2) == 0


def collide_layer(pop, pore):
    p0 = pop(0)
    sums = []
    diffs = []
    for pair in range(9):
        fwd = pop(2 * pair + 1)
        bwd = pop(2 * pair + 2)
        sums.append(fwd + bwd)
        diffs.append(fwd - bwd)
    density = p0
    for s in sums:
        density = density + s
    mom_z = diffs[0] + diffs[3] + diffs[4] + diffs[5] + diffs[6]
    mom_y = diffs[1] + diffs[3] - diffs[4] + diffs[7] + diffs[8]
    mom_x = diffs[2] + diffs[5] - diffs[6] + diffs[7] - diffs[8]
    inv = 1.0 / density
    u_z = mom_z * inv + RELAX_TIME * BODY_FORCE
    u_y = mom_y * inv
    u_x = mom_x * inv
    is_pore = pore > 0
    rate = 1.0 / RELAX_TIME
    keep_s = jnp.where(is_pore, 0.5 * (1.0 - rate), 0.5)
    keep_d = jnp.where(is_pore, 0.5 * (1.0 - rate), -0.5)
    scaled = jnp.where(is_pore, density * (rate / 36.0), 0.0)
    h_z, h_y, h_x = scaled * u_z, scaled * u_y, scaled * u_x
    q_zz, q_yy, q_xx = 4.5 * h_z * u_z, 4.5 * h_y * u_y, 4.5 * h_x * u_x
    base = scaled - (q_zz + q_yy + q_xx) * (1.0 / 3.0)
    m_z, m_y, m_x = 3.0 * h_z, 3.0 * h_y, 3.0 * h_x
    q_zy, q_zx, q_yx = 3.0 * m_z * u_y, 3.0 * m_z * u_x, 3.0 * m_y * u_x
    out = [(keep_s + keep_s) * p0 + 12.0 * base]
    evens = [
        2.0 * (base + q_zz),
        2.0 * (base + q_yy),
        2.0 * (base + q_xx),
    ]
    zy = base + q_zz + q_yy
    zx = base + q_zz + q_xx
    yx = base + q_yy + q_xx
    evens += [zy + q_zy, zy - q_zy, zx + q_zx, zx - q_zx, yx + q_yx, yx - q_yx]
    odds = [2.0 * m_z, 2.0 * m_y, 2.0 * m_x, m_z + m_y, m_z - m_y, m_z + m_x, m_z - m_x, m_y + m_x, m_y - m_x]
    for pair in range(9):
        even = keep_s * sums[pair] + evens[pair]
        odd = keep_d * diffs[pair] + odds[pair]
        out.append(even + odd)
        out.append(even - odd)
    return out


def stream_layer(r):
    width, x_width = r[0].shape
    shape = (width, x_width)
    r = list(r)
    for i, sign in ((5, 1), (11, 1), (14, 1), (15, 1), (18, 1), (6, -1), (12, -1), (13, -1), (16, -1), (17, -1)):
        r[i] = pltpu.roll(r[i], sign % x_width, 1)
    top = row_mask(shape, 0)
    bottom = row_mask(shape, width - 1)
    moved, edges = [], []
    for side, (plain, x_up, x_down, z_up, z_down) in enumerate(((3, 15, 17, 7, 10), (4, 18, 16, 9, 8))):
        both = r[plain] + r[x_up] + r[x_down]
        diff = r[x_up] - r[x_down]
        values = (both, diff, r[z_up], r[z_down])
        edge = width - 1 if side == 0 else 0
        edges.append([v[edge : edge + 1] for v in values])
        turn = 1 if side == 0 else width - 1
        moved.append([jnp.where(top if side == 0 else bottom, 0.0, pltpu.roll(v, turn, 0)) for v in values])
    (up_d, up_x, up_zu, up_zd), (dn_d, dn_x, dn_zu, dn_zd) = moved
    above = (r[1] + r[11] + r[13] + up_zu + dn_zu, up_zu - dn_zu, r[11] - r[13])
    here = (r[0] + r[5] + r[6] + up_d + dn_d, up_d - dn_d, r[5] - r[6] + up_x + dn_x)
    below = (r[2] + r[12] + r[14] + up_zd + dn_zd, up_zd - dn_zd, r[14] - r[12])
    return above, here, below, edges


def edge_kernel(
    pops, magnet, pore, wall, z_near, z_far, y_near, y_far, low_p, high_p, mag, por, wal, up, down, left, right, sems
):
    depth, width = por.shape[:2]
    pairs = [
        (pops.at[:, pl.ds(depth - 2, 2)], high_p),
        (pore, por),
        (pops.at[:, pl.ds(0, 2)], low_p),
        (wall, wal),
        (magnet, mag),
    ]
    copies = [pltpu.make_async_copy(src, dst, sems.at[i]) for i, (src, dst) in enumerate(pairs)]
    for copy in copies:
        copy.start()
    copies[1].wait()
    for face, held, copy, border, behind in ((up, high_p, 0, 1, 0), (down, low_p, 2, 0, 1)):
        copies[copy].wait()
        first = depth - 2 if face is up else 0

        def layer(at):
            return stream_layer(collide_layer(lambda i: held[i, at], por[first + at]))

        above, here, below, edges = layer(border)
        above_in, _, below_in, edges_in = layer(behind)
        cross, along = (above, above_in) if face is up else (below, below_in)
        sign = 1.0 if face is up else -1.0
        for j in range(3):
            face[j] = cross[j]
        face[3] = here[0] + along[0]
        face[4] = sign * along[0]
        face[5] = here[1] + along[1]
        face[6] = here[2] + along[2]
        diag = 2 if face is up else 3
        face[17] = jnp.zeros_like(face[17])
        for side in range(2):
            at = 4 * side
            face[17, at : at + 1, :] = edges[side][diag]
            face[17, at + 1 : at + 2, :] = edges[side][0] + edges_in[side][diag]
            face[17, at + 2 : at + 3, :] = sign * edges_in[side][diag]
            face[17, at + 3 : at + 4, :] = edges[side][1]
        if face is up:
            copies[3].wait()
            copies[4].wait()
        at, back = (depth - 1, depth - 2) if face is up else (0, 1)
        face[7:11] = mag[:, at]
        face[11:15] = mag[:, back]
        face[15] = por[at].astype(jnp.float32)
        face[16] = wal[at].astype(jnp.float32)

    def send(even, src, if_even, if_odd, sem):
        to_even = pltpu.make_async_copy(src, if_even, sem)
        to_odd = pltpu.make_async_copy(src, if_odd, sem)

        @pl.when(even)
        def _():
            to_even.start()

        @pl.when(jnp.logical_not(even))
        def _():
            to_odd.start()

        return to_even

    even_z, even_y = is_even("flow"), is_even("trans")
    sent = [
        send(even_z, up, z_near, z_far, sems.at[5]),
        send(even_z, down, z_far, z_near, sems.at[6]),
    ]

    def rows(z, carry):
        at = pl.ds(z, 1)
        for face, border, behind in ((right, width - 1, width - 2), (left, 0, 1)):
            for k in range(4):
                face[k, at, :] = mag[k, z, border : border + 1, :]
                face[4 + k, at, :] = mag[k, z, behind : behind + 1, :]
            face[8, at, :] = por[z, border : border + 1, :].astype(jnp.float32)
            face[9, at, :] = wal[z, border : border + 1, :].astype(jnp.float32)
        return carry

    lax.fori_loop(0, depth, rows, 0, unroll=6)
    sent += [
        send(even_y, right, y_near, y_far, sems.at[7]),
        send(even_y, left, y_far, y_near, sems.at[8]),
    ]
    for copy in sent:
        copy.wait()


def collide_kernel(pops, pore, acc, up, down, held, por, rows, sems):
    depth, width, x_width = por.shape
    shape = (width, x_width)
    chunks = sems.shape[0] - 1
    size = depth // chunks
    copies = [
        pltpu.make_async_copy(pops.at[:, pl.ds(c * size, size)], held.at[:, pl.ds(c * size, size)], sems.at[c])
        for c in range(chunks)
    ]
    pore_copy = pltpu.make_async_copy(pore, por, sems.at[chunks])
    pore_copy.start()
    for copy in copies:
        copy.start()
    acc[:, 0:2] = jnp.zeros((4, 2) + shape, jnp.float32)

    def layer(z, carry):
        above, here, below, edges = stream_layer(collide_layer(lambda i: held[i, z], por[z]))
        for side in range(2):
            for slot in range(4):
                rows[side, slot, pl.ds(z, 1), :] = edges[side][slot]
        acc[0, z + 2] = above[0]
        acc[1, z + 2] = above[0]
        acc[2, z + 2] = above[1]
        acc[3, z + 2] = above[2]
        acc[0, z + 1] = acc[0, z + 1] + here[0]
        acc[2, z + 1] = acc[2, z + 1] + here[1]
        acc[3, z + 1] = acc[3, z + 1] + here[2]
        acc[0, z] = acc[0, z] + below[0]
        acc[1, z] = acc[1, z] - below[0]
        acc[2, z] = acc[2, z] + below[1]
        acc[3, z] = acc[3, z] + below[2]
        return carry

    pore_copy.wait()
    for c in range(chunks):
        copies[c].wait()
        lax.fori_loop(c * size, (c + 1) * size, layer, 0, unroll=2)

    first = row_mask((depth, x_width), 0)
    final = row_mask((depth, x_width), depth - 1)
    for side, face in ((0, up), (1, down)):
        from_below = jnp.where(first, 0.0, pltpu.roll(rows[side, 2], 1, 0))
        from_above = jnp.where(final, 0.0, pltpu.roll(rows[side, 3], depth - 1, 0))
        face[0] = rows[side, 0] + from_below + from_above
        face[1] = from_below - from_above
        face[2] = rows[side, 1]
        face[7] = jnp.zeros_like(face[7])
        face[7, 0:1, :] = rows[side, 3, 0:1, :]
        face[7, 3:4, :] = rows[side, 2, depth - 1 : depth, :]

    def border(z, carry):
        for face, edge in ((up, width - 1), (down, 0)):
            for k in range(4):
                face[3 + k, pl.ds(z, 1), :] = acc[k, z + 1, edge : edge + 1, :]
        return carry

    lax.fori_loop(0, depth, border, 0, unroll=2)


def merge_kernel(got_near, got_far, up, down, near, far, low, high):
    depth = up.shape[1]
    width = low.shape[1]
    even_z = is_even("flow")
    low[...] = jnp.where(even_z, got_far[...], got_near[...])
    high[...] = jnp.where(even_z, got_near[...], got_far[...])

    def put(face, own, side, edge):
        face[...] = own[...]
        at = 4 * side
        for halo, z, sign, base, corner in ((low, 0, 1.0, 0, 6), (high, depth - 1, -1.0, 3, 10)):
            here = slice(z, z + 1)
            diag = halo[17, at : at + 1, :]
            face[0, here, :] = own[0, here, :] + diag
            face[1, here, :] = own[1, here, :] + sign * diag
            cross = halo[0, edge : edge + 1, :]
            face[3, here, :] = own[3, here, :] + cross
            face[4, here, :] = own[4, here, :] + sign * cross
            face[5, here, :] = own[5, here, :] + halo[1, edge : edge + 1, :]
            face[6, here, :] = own[6, here, :] + halo[2, edge : edge + 1, :]
            mine = own[7, base : base + 1, :]
            face[7, base : base + 1, :] = halo[17, at + 1 : at + 2, :] + mine
            face[7, base + 1 : base + 2, :] = halo[17, at + 2 : at + 3, :] - sign * mine
            face[7, base + 2 : base + 3, :] = halo[17, at + 3 : at + 4, :]
            for k in range(4):
                face[7, corner + k : corner + k + 1, :] = halo[7 + k, edge : edge + 1, :]

    even = is_even("trans")

    @pl.when(even)
    def _():
        put(near, up, 0, width - 1)
        put(far, down, 1, 0)

    @pl.when(jnp.logical_not(even))
    def _():
        put(near, down, 1, 0)
        put(far, up, 0, width - 1)


def coefficients(vel, pore, wall):
    half = [0.5 * v for v in vel]
    plain = DIFFUSION * pore
    center = (1.0 - 6.0 * DIFFUSION) * pore - SURFACE * (pore * wall)
    return center, [(plain - h, plain + h) for h in half]


def stencil(coef, center, z_pair, y_pair, x_width):
    mid, ((z_p, z_m), (y_p, y_m), (x_p, x_m)) = coef
    plus_x = pltpu.roll(center, x_width - 1, 1)
    minus_x = pltpu.roll(center, 1, 1)
    return (
        mid * center
        + (z_p * z_pair[0] + z_m * z_pair[1])
        + (y_p * y_pair[0] + y_m * y_pair[1])
        + (x_p * plus_x + x_m * minus_x)
    )


def rotate(values, cos, sin):
    out = []
    for k in range(2):
        re, im = values[2 * k], values[2 * k + 1]
        out.append(re * cos[k] + im * sin[k])
        out.append(im * cos[k] - re * sin[k])
    return out


def beside(center, row_low, row_high):
    width = center.shape[0]
    plus = jnp.where(row_mask(center.shape, width - 1), row_high, pltpu.roll(center, width - 1, 0))
    minus = jnp.where(row_mask(center.shape, 0), row_low, pltpu.roll(center, 1, 0))
    return plus, minus


def phases(table, z):
    return [table[0, z + 1], table[1, z + 1]], [table[2, z + 1], table[3, z + 1]]


def turned_pair(center):
    return pltpu.roll(center, center.shape[0] - 1, 0), pltpu.roll(center, 1, 0)


def inner_kernel(
    table, magnet, pore, wall, acc, low, high, near_m, far_m, near_w, far_w,
    vel_out, new_out, own, inner, ends, part, por, wal, mag, mid, vel, new, sems,
):
    depth, width, x_width = por.shape
    copies = [
        pltpu.make_async_copy(src, dst, sems.at[i])
        for i, (src, dst) in enumerate(((pore, por), (wall, wal), (magnet, mag)))
    ]
    for copy in copies:
        copy.start()
    even = is_even("trans")
    for planes, near, far in ((slice(0, 10), near_m, far_m), (slice(10, 18), near_w, far_w)):
        own[0, planes] = jnp.where(even, far[...], near[...])
        own[1, planes] = jnp.where(even, near[...], far[...])
    for copy in copies:
        copy.wait()

    def step(z, speed, pore_f, wall_f, center, plus, minus, put):
        coef = coefficients(speed, pore_f, wall_f)
        values = []
        for k in range(4):
            mid_k = center(k)
            values.append(stencil(coef, mid_k, (plus(k), minus(k)), turned_pair(mid_k), x_width))
        values = rotate(values, *phases(table, z))
        for k in range(4):
            put[k, z + 1 if put is mid else z] = values[k]
        return values

    def layer(z, extra, plus, minus):
        moments = [acc[k, z + 1] for k in range(4)]
        if extra is not None:
            halo, sign = extra
            moments = [
                moments[0] + halo[0],
                moments[1] + sign * halo[0],
                moments[2] + halo[1],
                moments[3] + halo[2],
            ]
        pore_f = por[z].astype(jnp.float32)
        scale = pore_f / moments[0]
        speed = [m * scale for m in moments[1:]]
        for j in range(3):
            vel[j, z] = speed[j]
        step(z, speed, pore_f, wal[z].astype(jnp.float32), lambda k: mag[k, z], plus, minus, mid)

    for halo, z, cross, border in ((low, -1, 0, 0), (high, depth, depth + 1, depth - 1)):
        scale = halo[15] / (halo[3] + acc[0, cross])
        speed = [(halo[4 + j] + acc[1 + j, cross]) * scale for j in range(3)]
        towards, behind = (lambda k: mag[k, border]), (lambda k: halo[11 + k])
        pair = (towards, behind) if z < 0 else (behind, towards)
        step(z, speed, halo[15], halo[16], lambda k: halo[7 + k], *pair, mid)

    layer(0, (low, 1.0), lambda k: mag[k, 1], lambda k: low[7 + k])

    def middle(z, carry):
        layer(z, None, lambda k: mag[k, z + 1], lambda k: mag[k, z - 1])
        return carry

    lax.fori_loop(1, depth - 1, middle, 0, unroll=4)
    layer(depth - 1, (high, -1.0), lambda k: high[7 + k], lambda k: mag[k, depth - 2])

    def second(z, totals):
        speed = [vel[j, z] for j in range(3)]
        pore_f, wall_f = por[z].astype(jnp.float32), wal[z].astype(jnp.float32)
        values = step(
            z, speed, pore_f, wall_f, lambda k: mid[k, z + 1], lambda k: mid[k, z + 2], lambda k: mid[k, z], new
        )
        return tuple(t + v for t, v in zip(totals, values))

    chunks = 6 if depth % 6 == 0 else 1
    size = depth // chunks
    totals = (jnp.zeros((width, x_width), jnp.float32),) * 4
    stores = [pltpu.make_async_copy(vel, vel_out, sems.at[3])]
    stores[0].start()
    for c in range(chunks):
        totals = lax.fori_loop(c * size, (c + 1) * size, second, totals, unroll=4)
        at = pl.ds(c * size, size)
        stores.append(pltpu.make_async_copy(new.at[:, at], new_out.at[:, at], sems.at[4 + c]))
        stores[-1].start()

    def rows(z, carry):
        at = pl.ds(z, 1)
        for side, one, two in ((0, 1, 2), (1, width - 2, width - 3)):
            for k in range(4):
                inner[side, k, at, :] = mid[k, z + 1, one : one + 1, :]
                inner[side, 4 + k, at, :] = mid[k, z + 1, two : two + 1, :]
            for j in range(3):
                inner[side, 8 + j, at, :] = vel[j, z, one : one + 1, :]
            inner[side, 11, at, :] = por[z, one : one + 1, :].astype(jnp.float32)
            inner[side, 12, at, :] = wal[z, one : one + 1, :].astype(jnp.float32)
        return carry

    lax.fori_loop(0, depth, rows, 0, unroll=2)
    line = lax.broadcasted_iota(jnp.int32, (width, x_width), 0)
    kept = jnp.logical_and(line >= 2, line < width - 2)
    part[...] = jnp.zeros_like(part)
    for k in range(4):
        for side, one in ((0, 1), (1, width - 2)):
            ends[side, k : k + 1, :] = mid[k, 0, one : one + 1, :]
            ends[side, 4 + k : 5 + k, :] = mid[k, depth + 1, one : one + 1, :]
        part[k : k + 1, :] = jnp.sum(jnp.where(kept, totals[k], 0.0), axis=0, keepdims=True)
    for copy in stores:
        copy.wait()


def border_kernel(
    table, wide, magnet, acc, low, high, own, inner, ends, part,
    got_near_m, got_far_m, got_near, got_far, vel_in, new_in,
    vel_out, mag_out, sums, inside, beside_m, beside_w, speeds, rows, corners, sems,
):
    depth, x_width = own.shape[2:]
    width = low.shape[1]
    shape = (width, x_width)
    loads = [
        pltpu.make_async_copy(magnet.at[:, pl.ds(0, 1)], inside.at[:, pl.ds(0, 1)], sems.at[0]),
        pltpu.make_async_copy(magnet.at[:, pl.ds(depth - 1, 1)], inside.at[:, pl.ds(1, 1)], sems.at[1]),
    ]
    for copy in loads:
        copy.start()
    even = is_even("trans")
    for pair, near, far in ((beside_m, got_near_m, got_far_m), (beside_w, got_near, got_far)):
        pair[0] = jnp.where(even, far[...], near[...])
        pair[1] = jnp.where(even, near[...], far[...])

    first = row_mask((depth, x_width), 0)
    final = row_mask((depth, x_width), depth - 1)
    cos = [jnp.concatenate([wide[k], wide[k]], axis=1) for k in range(2)]
    sin = [jnp.concatenate([wide[2 + k], wide[2 + k]], axis=1) for k in range(2)]

    def column(speed, pore_f, wall_f, center, end, y_pair):
        coef = coefficients(speed, pore_f, wall_f)
        values = []
        for k in range(4):
            low_end, high_end = end(k)
            mid_k = center(k)
            plus = jnp.where(final, high_end, pltpu.roll(mid_k, depth - 1, 0))
            minus = jnp.where(first, low_end, pltpu.roll(mid_k, 1, 0))
            values.append(stencil(coef, mid_k, (plus, minus), y_pair(k), x_width))
        return rotate(values, cos, sin)

    def flow(moments, cross, sign, pore_f):
        scale = pore_f / (moments(0) + cross(0))
        return [
            (moments(1) + cross(1)) * scale,
            (moments(2) + sign * cross(0)) * scale,
            (moments(3) + cross(2)) * scale,
        ]

    edges = (0, width - 1)
    orders = ((lambda a, b: (a, b)), (lambda a, b: (b, a)))
    stores = []
    for side, edge in enumerate(edges):
        face, mine, late = beside_m.at[side], own.at[side], beside_w.at[side]
        sign = -1.0 if side == 0 else 1.0
        order = orders[side]
        speed = flow(lambda j: late[3 + j], lambda j: mine[10 + j], sign, face[8])
        outer = column(
            speed,
            face[8],
            face[9],
            lambda k: face[k],
            lambda k: (late[7, 6 + k : 7 + k, :], late[7, 10 + k : 11 + k, :]),
            lambda k: order(mine[k], face[4 + k]),
        )
        speed = flow(lambda j: mine[13 + j], lambda j: late[j], -sign, mine[8])
        border = column(
            speed,
            mine[8],
            mine[9],
            lambda k: mine[k],
            lambda k: (low[7 + k, edge : edge + 1, :], high[7 + k, edge : edge + 1, :]),
            lambda k: order(mine[4 + k], face[k]),
        )
        for k in range(4):
            rows[side, 0, k] = outer[k]
            rows[side, 1, k] = border[k]
        for j in range(3):
            speeds[side, j] = speed[j]
        stores.append(pltpu.make_async_copy(speeds.at[side], vel_out.at[:, :, edge], sems.at[2 + side]))
        stores[-1].start()

    for copy in loads:
        copy.wait()
    top = row_mask(shape, 0)
    bottom = row_mask(shape, width - 1)
    for halo, z, cross, base, corner, at_end in ((low, -1, 0, 0, 6, 0), (high, depth, depth + 1, 3, 10, 1)):
        d_l, z_l, x_l = [beside_w[0, 7, base + j : base + j + 1, :] for j in range(3)]
        d_r, z_r, x_r = [beside_w[1, 7, base + j : base + j + 1, :] for j in range(3)]
        density = halo[3] + acc[0, cross] + jnp.where(top, d_l, jnp.where(bottom, d_r, 0.0))
        m_z = halo[4] + acc[1, cross] + jnp.where(top, z_l, jnp.where(bottom, z_r, 0.0))
        m_y = halo[5] + acc[2, cross] + jnp.where(top, d_l, jnp.where(bottom, -d_r, 0.0))
        m_x = halo[6] + acc[3, cross] + jnp.where(top, x_l, jnp.where(bottom, x_r, 0.0))
        scale = halo[15] / density
        coef = coefficients([m_z * scale, m_y * scale, m_x * scale], halo[15], halo[16])
        values = []
        for k in range(4):
            center = halo[7 + k]
            z_pair = (inside[k, at_end], halo[11 + k])
            z_pair = z_pair if z < 0 else z_pair[::-1]
            at = slice(corner + k, corner + k + 1)
            y_pair = beside(center, beside_w[0, 7, at, :], beside_w[1, 7, at, :])
            values.append(stencil(coef, center, z_pair, y_pair, x_width))
        for k, value in enumerate(rotate(values, *phases(table, z))):
            for side, edge in enumerate(edges):
                at = 4 * at_end + k
                corners[side, at : at + 1, :] = value[edge : edge + 1]

    totals = [part[k : k + 1, :] for k in range(4)]
    for side, edge in enumerate(edges):
        mine, own_in, order = own.at[side], inner.at[side], orders[side]
        for row, values in enumerate(
            (
                column(
                    [speeds[side, j] for j in range(3)],
                    mine[8],
                    mine[9],
                    lambda k: rows[side, 1, k],
                    lambda k: (corners[side, k : k + 1, :], corners[side, 4 + k : 5 + k, :]),
                    lambda k: order(own_in[k], rows[side, 0, k]),
                ),
                column(
                    [own_in[8 + j] for j in range(3)],
                    own_in[11],
                    own_in[12],
                    lambda k: own_in[k],
                    lambda k: (ends[side, k : k + 1, :], ends[side, 4 + k : 5 + k, :]),
                    lambda k: order(own_in[4 + k], rows[side, 1, k]),
                ),
            )
        ):
            for k in range(4):
                rows[side, 2 + row, k] = values[k]
                totals[k] = totals[k] + jnp.sum(values[k], axis=0, keepdims=True)
            at = edge + (row if side == 0 else -row)
            stores.append(
                pltpu.make_async_copy(rows.at[side, 2 + row], mag_out.at[:, :, at], sems.at[4 + 2 * side + row])
            )
            stores[-1].start()
    lane = lax.broadcasted_iota(jnp.int32, sums.shape, 1)
    line = jnp.zeros(sums.shape, jnp.float32)
    for k in range(4):
        line = jnp.where(lane == k, jnp.sum(totals[k], axis=1, keepdims=True), line)
    sums[...] = line
    for copy in stores:
        copy.wait()


VMEM = pl.BlockSpec(memory_space=pltpu.VMEM)
SMEM = pl.BlockSpec(memory_space=pltpu.SMEM)
HBM = pl.BlockSpec(memory_space=pltpu.HBM)


def struct(*shape):
    return jax.ShapeDtypeStruct(shape, jnp.float32)


def floats(*shape):
    return pltpu.VMEM(shape, jnp.float32)


def ints(*shape):
    return pltpu.VMEM(shape, jnp.int32)


def params(mib):
    return pltpu.CompilerParams(vmem_limit_bytes=mib * MIB)


def edge_faces(pops, magnet, pore, wall):
    depth, width, x_width = pore.shape
    return pl.pallas_call(
        edge_kernel,
        in_specs=[HBM] * 4,
        out_specs=[HBM] * 4,
        out_shape=[struct(18, width, x_width)] * 2 + [struct(10, depth, x_width)] * 2,
        scratch_shapes=[
            floats(19, 2, width, x_width),
            floats(19, 2, width, x_width),
            floats(4, depth, width, x_width),
            ints(depth, width, x_width),
            ints(depth, width, x_width),
            floats(18, width, x_width),
            floats(18, width, x_width),
            floats(10, depth, x_width),
            floats(10, depth, x_width),
            pltpu.SemaphoreType.DMA((9,)),
        ],
        compiler_params=params(60),
        name="edge_faces",
    )(pops, magnet, pore, wall)


def collide(pops, pore):
    depth, width, x_width = pore.shape
    chunks = 12 if depth % 24 == 0 else 1
    return pl.pallas_call(
        collide_kernel,
        in_specs=[HBM] * 2,
        out_specs=[VMEM] * 3,
        out_shape=[struct(4, depth + 2, width, x_width)] + [struct(8, depth, x_width)] * 2,
        scratch_shapes=[
            floats(19, depth, width, x_width),
            ints(depth, width, x_width),
            floats(2, 4, depth, x_width),
            pltpu.SemaphoreType.DMA((chunks + 1,)),
        ],
        compiler_params=params(48),
        cost_estimate=pl.CostEstimate(flops=20_000_000, bytes_accessed=12_000_000, transcendentals=0),
        name="collide",
    )(pops, pore)


def merge(got_near, got_far, up, down):
    return pl.pallas_call(
        merge_kernel,
        in_specs=[VMEM] * 4,
        out_specs=[VMEM] * 4,
        out_shape=[struct(*up.shape)] * 2 + [struct(*got_near.shape)] * 2,
        compiler_params=params(8),
        name="merge",
    )(got_near, got_far, up, down)


def inner_steps(table, magnet, pore, wall, acc, low, high, *faces):
    depth, width, x_width = pore.shape
    return pl.pallas_call(
        inner_kernel,
        in_specs=[SMEM] + [HBM] * 3 + [VMEM] * (3 + len(faces)),
        out_specs=[HBM] * 2 + [VMEM] * 4,
        out_shape=[
            struct(3, depth, width, x_width),
            struct(4, depth, width, x_width),
            struct(2, 18, depth, x_width),
            struct(2, 13, depth, x_width),
            struct(2, 8, x_width),
            struct(8, x_width),
        ],
        scratch_shapes=[
            ints(depth, width, x_width),
            ints(depth, width, x_width),
            floats(4, depth, width, x_width),
            floats(4, depth + 2, width, x_width),
            floats(3, depth, width, x_width),
            floats(4, depth, width, x_width),
            pltpu.SemaphoreType.DMA((10,)),
        ],
        compiler_params=params(24),
        cost_estimate=pl.CostEstimate(flops=40_000_000, bytes_accessed=9_000_000, transcendentals=0),
        name="inner_steps",
    )(table, magnet, pore, wall, acc, low, high, *faces)


def border_rows(table, wide, magnet, *rest):
    depth, width, x_width = magnet.shape[1:]
    count = len(rest) - 2
    return pl.pallas_call(
        border_kernel,
        in_specs=[SMEM, VMEM, HBM] + [VMEM] * count + [HBM] * 2,
        out_specs=[HBM, HBM, VMEM],
        out_shape=[struct(3, depth, width, x_width), struct(4, depth, width, x_width), struct(1, 128)],
        input_output_aliases={3 + count: 0, 4 + count: 1},
        scratch_shapes=[
            floats(4, 2, width, x_width),
            floats(2, 10, depth, x_width),
            floats(2, 8, depth, x_width),
            floats(2, 3, depth, x_width),
            floats(2, 4, 4, depth, x_width),
            floats(2, 8, x_width),
            pltpu.SemaphoreType.DMA((8,)),
        ],
        compiler_params=params(16),
        name="border_rows",
    )(table, wide, magnet, *rest)


def swap(value, axis, near):
    count = lax.axis_size(axis)
    step = 1 if near else -1
    return lax.ppermute(value, axis, [(i, (i + (step if i % 2 == 0 else -step)) % count) for i in range(count)])


def phase_tables(start, depth, extent):
    layers = jnp.remainder(start + jnp.arange(-1, depth + 1, dtype=jnp.int32), extent)
    coords = layers.astype(jnp.float32)
    wave_numbers = jnp.array([Q_LOW, Q_HIGH], jnp.float32)
    angles = 2.0 * math.pi * wave_numbers[:, None] * coords[None, :] / extent
    return jnp.concatenate([jnp.cos(angles), jnp.sin(angles)], axis=0)


def sum_over(value, axes):
    count = math.prod(lax.axis_size(axis) for axis in axes)
    copies = jnp.broadcast_to(value[None], (count,) + value.shape)
    return jnp.sum(lax.all_to_all(copies, axes, 0, 0), axis=(0, 1))


def local(populations, magnetization, pore, wall):
    _, depth, width, x_width = populations.shape
    flow_count = lax.axis_size("flow")
    trans_count = lax.axis_size("trans")
    extent = depth * flow_count
    magnet = magnetization.reshape(4, depth, width, x_width)
    table = phase_tables(lax.axis_index("flow") * depth, depth, extent)
    wide = jnp.broadcast_to(table[:, 1:-1, None], (4, depth, 128))

    near_z, far_z, near_m, far_m = edge_faces(populations, magnet, pore, wall)
    near_m, table, wide = lax.optimization_barrier((near_m, table, wide))
    got_near_z = swap(near_z, "flow", True)
    got_far_z = swap(far_z, "flow", False)
    got_near_m = swap(near_m, "trans", True)
    got_far_m = swap(far_m, "trans", False)
    acc, up, down = collide(populations, pore)
    near_w, far_w, low, high = merge(got_near_z, got_far_z, up, down)
    got_near_w = swap(near_w, "trans", True)
    got_far_w = swap(far_w, "trans", False)
    velocity, magnet_out, own, inner, ends, part = inner_steps(
        table, magnet, pore, wall, acc, low, high, near_m, far_m, near_w, far_w
    )
    velocity, magnet, sums = border_rows(
        table, wide, magnet, acc, low, high, own, inner, ends, part,
        got_near_m, got_far_m, got_near_w, got_far_w, velocity, magnet_out,
    )
    totals = sum_over(sums, ("flow", "trans"))
    signal = totals[:4].reshape(2, 2) / math.sqrt(extent * width * trans_count * x_width)
    return (velocity, magnet.reshape(magnetization.shape), signal)


def solution(mesh):
    placed = (
        P(None, "flow", "trans", None),
        P(None, None, "flow", "trans", None),
        P("flow", "trans", None),
        P("flow", "trans", None),
    )
    return jax.shard_map(
        local,
        mesh=mesh,
        in_specs=placed,
        out_specs=(P(None, "flow", "trans", None), P(None, None, "flow", "trans", None), P()),
        check_vma=False,
    )
```
